32 devices in a mesh: facet: 8 (over y, x, core), strip: 4 (over z).
Axes of the slice: x: 2, y: 2, z: 4, core: 2. Of those that a mesh axis runs over, the one named last changes fastest.
Arguments:
- facet_pixels: bfloat16 [2, 8, 512, 4096], P(None, 'facet', 'strip'), may hold values from -6 to 6
- facet_offsets: int32 [8, 2], P('facet'), may hold values from 0 to 65535
- subgrid_offsets: int32 [2, 2], replicated, may hold values from 0 to 65023
Outputs:
- subgrid: float32 [512, 2, 2, 512], P('strip', None, None, 'facet')
The draws below stay inside these ranges and needn't reach their ends.
All inputs are finite; a program needn't handle non-finite values.
Results may differ from the reference program's by a relative error of at most 0.0074.
Values may be sent and summed in bfloat16 or wider, within the bound.
A program may use at most 64 MiB of HBM per device.

```python
import math
import jax
import jax.numpy as jnp
from jax import lax

IMAGE_N = 65536
FACET_W = 4096
FREQ = 512
ROW_FREQ = 512
COLUMNS = 2
FACETS = 8
FACET_ROWS = 512


def set_ends(entries, stream_key, low, top_value):
    longest = entries.shape.index(max(entries.shape))
    spots = []
    for shift in (0, 1):
        where = [jax.random.randint(jax.random.fold_in(stream_key, axis), (), 0, length) for axis, length in enumerate(entries.shape)]
        where[longest] = (where[longest] + shift) % entries.shape[longest]
        spots.append(tuple(where))
    return entries.at[spots[0]].set(low).at[spots[1]].set(top_value)


def levels(key, dims, pieces, low, largest):
    factor_of = 1.0
    for axis_at, parts in pieces:
        steps = jax.random.uniform(jax.random.fold_in(jax.random.fold_in(key, 6), axis_at), (parts,), jnp.float32, low / len(pieces), largest / len(pieces))
        factor_of = factor_of * jnp.repeat(jnp.exp(steps), dims[axis_at] // parts).reshape((-1,) + (1,) * (len(dims) - 1 - axis_at))
    return factor_of


def normal_values(key, shape, width, reach, split=(), kind=jnp.bfloat16):
    drawn = jax.random.normal(key, shape, jnp.float32) * width
    if len(split) > 0:
        drawn = levels(key, shape, split, -0.22, 0.18) * drawn
    return jnp.clip(drawn, min=-reach, max=reach).astype(kind)


def setup_inputs(seed: int = 0) -> dict:
    arg_keys = jax.random.split(jax.random.key(seed), 4)
    return {
        "facet_pixels": normal_values(arg_keys[0], (2, FACETS, FACET_ROWS, FACET_W), 1.0, 6.0, ((1, 8), (2, 4))),
        "facet_offsets": set_ends(jax.random.randint(arg_keys[1], (FACETS, 2), 0, IMAGE_N), jax.random.fold_in(arg_keys[1], 1), 0, IMAGE_N - 1).astype(jnp.int32),
        "subgrid_offsets": set_ends(jax.random.randint(arg_keys[2], (COLUMNS, 2), 0, IMAGE_N - max(FREQ, ROW_FREQ)), jax.random.fold_in(arg_keys[2], 1), 0, (IMAGE_N - max(FREQ, ROW_FREQ)) - 1).astype(jnp.int32),
    }


def phase_mod(offset, freq, modulus):
    high = offset // 256
    low = offset % 256
    return (high * (256 * freq % modulus) + low * freq) % modulus

def twiddle(product, modulus):
    angle = 2.0 * math.pi / modulus * product.astype(jnp.float32)
    return (jnp.cos(angle), -jnp.sin(angle))

def bf_tables(product, modulus):
    cosine, sine = twiddle(product, modulus)
    return (cosine.astype(jnp.bfloat16), sine.astype(jnp.bfloat16), (cosine + sine).astype(jnp.bfloat16))

def reference(facet_pixels, facet_offsets, subgrid_offsets):
    col_freq = subgrid_offsets[:, 0][:, None] + jnp.arange(FREQ, dtype=jnp.int32)[None, :]
    row_freq = subgrid_offsets[:, 1][:, None] + jnp.arange(ROW_FREQ, dtype=jnp.int32)[None, :]
    pixel_col = jnp.arange(FACET_W, dtype=jnp.int32)
    col_product = (pixel_col[:, None, None] * col_freq[None, :, :] % IMAGE_N).reshape(FACET_W, COLUMNS * FREQ)
    col_tables = bf_tables(col_product, IMAGE_N)
    pixel_row = jnp.arange(FACET_ROWS, dtype=jnp.int32)
    row_product = row_freq[:, :, None] * pixel_row[None, None, :] % IMAGE_N
    row_tables = bf_tables(row_product, IMAGE_N)
    scale = 1.0 / math.sqrt(FACET_W * FACET_ROWS * FACETS)

    def one_facet(index, running):
        pixels = lax.dynamic_index_in_dim(facet_pixels, index, 1, keepdims=False)
        offsets = lax.dynamic_index_in_dim(facet_offsets, index, 0, keepdims=False)
        pixels_real = pixels[0]
        pixels_imag = pixels[1]
        pixel_sum = (pixels_real.astype(jnp.float32) + pixels_imag.astype(jnp.float32)).astype(jnp.bfloat16)
        term_one = jnp.dot(pixels_real, col_tables[0], preferred_element_type=jnp.float32)
        term_two = jnp.dot(pixels_imag, col_tables[1], preferred_element_type=jnp.float32)
        term_three = jnp.dot(pixel_sum, col_tables[2], preferred_element_type=jnp.float32)
        y_real = (term_one - term_two).astype(jnp.bfloat16)
        y_imag = (term_three - term_one - term_two).astype(jnp.bfloat16)
        y_real, y_imag = lax.optimization_barrier((y_real, y_imag))
        y_sum = (y_real.astype(jnp.float32) + y_imag.astype(jnp.float32)).astype(jnp.bfloat16)
        y_real = y_real.reshape(FACET_ROWS, COLUMNS, FREQ).astype(jnp.float32)
        y_imag = y_imag.reshape(FACET_ROWS, COLUMNS, FREQ).astype(jnp.float32)
        y_sum = y_sum.reshape(FACET_ROWS, COLUMNS, FREQ).astype(jnp.float32)
        part_one = jnp.einsum('cir,rcm->icm', row_tables[0].astype(jnp.float32), y_real)
        part_two = jnp.einsum('cir,rcm->icm', row_tables[1].astype(jnp.float32), y_imag)
        part_three = jnp.einsum('cir,rcm->icm', row_tables[2].astype(jnp.float32), y_sum)
        z_real = part_one - part_two
        z_imag = part_three - part_one - part_two
        col_part = phase_mod(offsets[0], col_freq, IMAGE_N)
        row_part = phase_mod(offsets[1], row_freq, IMAGE_N)
        total = jnp.transpose((row_part[:, :, None] + col_part[:, None, :]) % IMAGE_N, (1, 0, 2))
        cosine, sine = twiddle(total, IMAGE_N)
        out_real = scale * (z_real * cosine - z_imag * sine)
        out_imag = scale * (z_real * sine + z_imag * cosine)
        return running + jnp.stack([out_real, out_imag], axis=1)
    start_value = jnp.zeros((ROW_FREQ, 2, COLUMNS, FREQ), jnp.float32)
    return lax.fori_loop(0, FACETS, one_facet, start_value)
```

```python
import functools
import math

import jax
import jax.numpy as jnp
import ml_dtypes
import numpy as np
from jax import lax
from jax.experimental import pallas as pl
from jax.experimental.pallas import tpu as pltpu
from jax.sharding import PartitionSpec as P

IMAGE_N = 65536
FREQ = 512
ROW_FREQ = 512
COLUMNS = 2
LANES = 128
CHUNK = 256
BF = jnp.bfloat16
F32 = jnp.float32
MESH = pl.DeviceIdType.MESH


def half_tables(count_a, count_b, step_a):
    a = 2 * np.arange(count_a, dtype=np.int64) + step_a
    b = 2 * np.arange(count_b, dtype=np.int64) + 1
    t = (a[:, None] * b[None, :]) % (4 * IMAGE_N)
    angle = 2.0 * np.pi * t / (4 * IMAGE_N)
    return np.cos(angle), np.sin(angle)


def cos_sin(product, modulus):
    t = (product + modulus // 2) & (modulus - 1)
    h = (t - modulus // 2).astype(F32) * (math.pi / modulus)
    h2 = h * h
    s = jnp.full_like(h, 1.0 / math.factorial(13))
    c = jnp.full_like(h, -1.0 / math.factorial(14))
    for n in range(11, 0, -2):
        s = s * h2 + (-1.0) ** ((n - 1) // 2) / math.factorial(n)
    for n in range(12, -1, -2):
        c = c * h2 + (-1.0) ** (n // 2) / math.factorial(n)
    s = s * h
    return 1.0 - 2.0 * s * s, 2.0 * s * c


def iota(shape, dim):
    return lax.broadcasted_iota(jnp.int32, shape, dim)


def dot(a, b):
    return jnp.dot(a, b, preferred_element_type=F32)


def kernel(
    facets, strips,
    fo_ref, so_ref, x_hbm, ct_hbm, st_hbm, rc_hbm, rs_hbm,
    out_ref,
    x, ct, st, rc, rs, evod, ysend, yrecv, tc, ts, off_send, off_recv, zsend, zrecv,
    load_sem, y_ssem, y_rsem, o_ssem, o_rsem, z_ssem, z_rsem,
):
    f_me = lax.axis_index("facet")
    s_me = lax.axis_index("strip")
    rows, width = x.shape[1], x.shape[2]
    half_k = width // 2
    half_m = FREQ // 2
    half_i = ROW_FREQ // 2
    mb = FREQ // facets
    ib = ROW_FREQ // strips
    chunks = half_k // CHUNK
    scale = 1.0 / math.sqrt(width * rows * strips * facets)

    loads = []

    def load(src, dst):
        copy = pltpu.make_async_copy(src, dst, load_sem.at[len(loads)])
        copy.start()
        loads.append(copy)
        return copy

    x_low, x_high = [], []
    for j in range(chunks):
        low = pl.ds((chunks - 1 - j) * CHUNK, CHUNK)
        high = pl.ds(half_k + j * CHUNK, CHUNK)
        x_low.append(load(x_hbm.at[:, 0, :, low], x.at[:, :, low]))
        x_high.append(load(x_hbm.at[:, 0, :, high], x.at[:, :, high]))
    ct_load = load(ct_hbm, ct)
    st_load = load(st_hbm, st)
    rc_load = load(rc_hbm, rc)
    rs_load = load(rs_hbm, rs)

    facet_peers = [lax.rem(f_me + d, facets) for d in range(1, facets)]
    strip_peers = [lax.rem(s_me + d, strips) for d in range(1, strips)]
    barrier = pltpu.get_barrier_semaphore()
    for peer in facet_peers:
        pl.semaphore_signal(barrier, inc=1, device_id=(peer, s_me), device_id_type=MESH)
    for peer in strip_peers:
        pl.semaphore_signal(barrier, inc=1, device_id=(f_me, peer), device_id_type=MESH)

    fx = fo_ref[0, 0]
    fy = fo_ref[0, 1]
    u0 = [so_ref[c, 0] for c in range(COLUMNS)]
    w0 = [so_ref[c, 1] for c in range(COLUMNS)]

    off_send[...] = jnp.full(off_send.shape, fy, jnp.int32)
    off_recv[f_me] = off_send[...]

    pieces = half_k // LANES
    a_index = iota((pieces, LANES), 0) * LANES + iota((pieces, LANES), 1)
    pq = [
        cos_sin((2 * a_index + 1) * (2 * u0[c] + (FREQ - 1)), 4 * IMAGE_N)
        for c in range(COLUMNS)
    ]

    row = iota((8, half_m), 0)
    lane = iota((8, half_m), 1)
    first = jnp.where(row < 2, u0[0], u0[1])
    freq = first + jnp.where((row & 1) == 0, half_m + lane, half_m - 1 - lane)
    hc, hs = cos_sin((2 * fx + (width - 1)) * freq, 2 * IMAGE_N)
    hc, hs = hc * scale, hs * scale

    padded = -(-rows // LANES) * LANES
    row = iota((8, padded), 0)
    first = jnp.where(row == 0, w0[0], w0[1])
    pixel_row = s_me * rows + iota((8, padded), 1) + fy
    gc, gs = cos_sin((2 * first + (ROW_FREQ - 1)) * pixel_row, 2 * IMAGE_N)
    gc, gs = jnp.transpose(gc), jnp.transpose(gs)

    flip = (iota((CHUNK, CHUNK), 0) + iota((CHUNK, CHUNK), 1) == CHUNK - 1).astype(F32).astype(BF)

    for j in range(chunks):
        cols = pl.ds(j * CHUNK, CHUNK)
        x_low[j].wait()
        x_high[j].wait()
        low = x[:, :, pl.ds((chunks - 1 - j) * CHUNK, CHUNK)].reshape(2 * rows, CHUNK)
        high = x[:, :, pl.ds(half_k + j * CHUNK, CHUNK)].reshape(2 * rows, CHUNK).astype(F32)
        low = dot(low, flip)
        even = high + low
        odd = high - low
        er, ei, odr, odi = even[:rows], even[rows:], odd[:rows], odd[rows:]
        first = j * (CHUNK // LANES)
        for c in range(COLUMNS):
            p, q = (
                jnp.concatenate(
                    [part[first + n : first + n + 1] for n in range(CHUNK // LANES)], axis=1
                )
                for part in pq[c]
            )
            evod[c, 0, :rows, cols] = (er * p + odi * q).astype(BF)
            evod[c, 0, rows:, cols] = (ei * p - odr * q).astype(BF)
            evod[c, 1, :rows, cols] = (odr * p + ei * q).astype(BF)
            evod[c, 1, rows:, cols] = (odi * p - er * q).astype(BF)

    pl.semaphore_wait(barrier, facets - 1 + strips - 1)

    def off_copy(d):
        return pltpu.make_async_remote_copy(
            src_ref=off_send,
            dst_ref=off_recv.at[f_me],
            send_sem=o_ssem.at[d - 1],
            recv_sem=o_rsem.at[d - 1],
            device_id=(facet_peers[d - 1], s_me),
            device_id_type=MESH,
        )

    def y_copy(c, d):
        return pltpu.make_async_remote_copy(
            src_ref=ysend.at[c, facet_peers[d - 1]],
            dst_ref=yrecv.at[c, f_me],
            send_sem=y_ssem.at[c, d - 1],
            recv_sem=y_rsem.at[c, d - 1],
            device_id=(facet_peers[d - 1], s_me),
            device_id_type=MESH,
        )

    def z_copy(c, d):
        return pltpu.make_async_remote_copy(
            src_ref=zsend.at[c, strip_peers[d - 1]],
            dst_ref=zrecv.at[c, d - 1],
            send_sem=z_ssem.at[c, d - 1],
            recv_sem=z_rsem.at[c, d - 1],
            device_id=(f_me, strip_peers[d - 1]),
            device_id_type=MESH,
        )

    off_copies = [off_copy(d) for d in range(1, facets)]
    for copy in off_copies:
        copy.start()

    ct_load.wait()
    st_load.wait()
    y_copies = []
    for c in range(COLUMNS):
        pp = dot(evod[c, 0], ct[...])
        qq = dot(evod[c, 1], st[...])
        halves = []
        for sign in (0, 1):
            if sign == 0:
                yr = pp[:rows] + qq[rows:]
                yi = pp[rows:] - qq[:rows]
            else:
                yr = pp[:rows] - qq[rows:]
                yi = pp[rows:] + qq[:rows]
            hcr, hsr = hc[2 * c + sign : 2 * c + sign + 1], hs[2 * c + sign : 2 * c + sign + 1]
            gcr, gsr = gc[:rows, c : c + 1], gs[:rows, c : c + 1]
            a = gcr * hcr - gsr * hsr
            b = gcr * hsr + gsr * hcr
            halves.append(((yr * a + yi * b).astype(BF), (yi * a - yr * b).astype(BF)))
        for f in range(facets):
            if f >= facets // 2:
                yr, yi = halves[0]
                start = mb * f - half_m
            else:
                yr, yi = halves[1]
                start = half_m - mb * (f + 1)
            ysend[c, f] = jnp.concatenate(
                [yr[:, start : start + mb], yi[:, start : start + mb]], axis=1
            )
        copies = [y_copy(c, d) for d in range(1, facets)]
        for copy in copies:
            copy.start()
        y_copies.append(copies)
        yrecv[c, f_me] = ysend[c, f_me]

    for copy in off_copies:
        copy.wait_recv()
    rc_load.wait()
    rs_load.wait()
    offs = jnp.concatenate([off_recv[:, 0, :]] * (half_i // LANES), axis=1)
    phc, phs = cos_sin(
        (2 * iota((facets, half_i), 1) + 1) * (offs + s_me * rows), 2 * IMAGE_N
    )
    phc, phs = jnp.transpose(phc), jnp.transpose(phs)
    base_c, base_s = rc[...], rs[...]
    for f in range(facets):
        pc, ps = phc[:, f : f + 1], phs[:, f : f + 1]
        tc[:, f * rows : (f + 1) * rows] = (base_c * pc - base_s * ps).astype(BF)
        ts[:, f * rows : (f + 1) * rows] = (base_s * pc + base_c * ps).astype(BF)

    src, dst = iota((2 * mb, 2 * mb), 0), iota((2 * mb, 2 * mb), 1)
    same_part = (src >= mb) == (dst >= mb)
    mirrored = (src + dst - jnp.where(dst >= mb, 2 * mb, 0)) == mb - 1
    lower = jnp.where(f_me < facets // 2, 1, 0)
    picked = jnp.where(lower == 1, jnp.where(same_part & mirrored, 1, 0), jnp.where(src == dst, 1, 0))
    order = picked.astype(F32).astype(BF)

    z_copies = []
    for c in range(COLUMNS):
        for copy in y_copies[c]:
            copy.wait_recv()
        y = yrecv[c].reshape(facets * rows, 2 * mb)
        aa = dot(tc[...], y)
        bb = dot(ts[...], y)
        turned = jnp.concatenate([bb[:, mb:], -bb[:, :mb]], axis=1)
        upper_rows = dot((aa + turned).astype(BF), order).astype(BF)
        lower_rows = dot(flip, (aa - turned).astype(BF)).astype(BF)
        lower_rows = dot(lower_rows, order).astype(BF)
        z = jnp.concatenate([lower_rows, upper_rows], axis=0)
        zsend[c] = z.reshape(strips, ib, 2 * mb)
        copies = [z_copy(c, d) for d in range(1, strips)]
        for copy in copies:
            copy.start()
        z_copies.append(copies)

    totals = []
    for c in range(COLUMNS):
        total = zsend[c, s_me].astype(F32)
        for d in range(1, strips):
            z_copies[c][d - 1].wait_recv()
            total += zrecv[c, d - 1].astype(F32)
        totals.append(total)
    out_ref[...] = jnp.concatenate(
        [totals[0][:, :mb], totals[1][:, :mb], totals[0][:, mb:], totals[1][:, mb:]], axis=1
    )
    for copy in off_copies + y_copies[0] + y_copies[1] + z_copies[0] + z_copies[1]:
        copy.wait_send()


def per_device(facet_pixels, facet_offsets, subgrid_offsets):
    rows, width = facet_pixels.shape[2], facet_pixels.shape[3]
    facets, strips = lax.axis_size("facet"), lax.axis_size("strip")
    mb, ib = FREQ // facets, ROW_FREQ // strips
    half_k, half_m, half_i = width // 2, FREQ // 2, ROW_FREQ // 2
    ct, st = (t.astype(ml_dtypes.bfloat16) for t in half_tables(half_k, half_m, 1))
    rc, rs = (
        np.ascontiguousarray(t.T.astype(np.float32)) for t in half_tables_rows(rows, half_i)
    )
    loads = 2 * (half_k // CHUNK) + 4
    dma = pltpu.SemaphoreType.DMA
    flops = 2 * (4 * 2 * rows * half_k * half_m + 4 * half_i * facets * rows * 2 * mb)
    out = pl.pallas_call(
        functools.partial(kernel, facets, strips),
        out_shape=jax.ShapeDtypeStruct((ib, 4 * mb), F32),
        in_specs=[pl.BlockSpec(memory_space=pltpu.SMEM)] * 2
        + [pl.BlockSpec(memory_space=pl.ANY)] * 5,
        out_specs=pl.BlockSpec(memory_space=pltpu.VMEM),
        scratch_shapes=[
            pltpu.VMEM((2, rows, width), BF),
            pltpu.VMEM((half_k, half_m), BF),
            pltpu.VMEM((half_k, half_m), BF),
            pltpu.VMEM((half_i, rows), F32),
            pltpu.VMEM((half_i, rows), F32),
            pltpu.VMEM((COLUMNS, 2, 2 * rows, half_k), BF),
            pltpu.VMEM((COLUMNS, facets, rows, 2 * mb), BF),
            pltpu.VMEM((COLUMNS, facets, rows, 2 * mb), BF),
            pltpu.VMEM((half_i, facets * rows), BF),
            pltpu.VMEM((half_i, facets * rows), BF),
            pltpu.VMEM((8, LANES), jnp.int32),
            pltpu.VMEM((facets, 8, LANES), jnp.int32),
            pltpu.VMEM((COLUMNS, strips, ib, 2 * mb), BF),
            pltpu.VMEM((COLUMNS, strips - 1, ib, 2 * mb), BF),
            dma((loads,)),
            dma((COLUMNS, facets - 1)),
            dma((COLUMNS, facets - 1)),
            dma((facets - 1,)),
            dma((facets - 1,)),
            dma((COLUMNS, strips - 1)),
            dma((COLUMNS, strips - 1)),
        ],
        compiler_params=pltpu.CompilerParams(
            collective_id=0, has_side_effects=True, vmem_limit_bytes=40 * 1024 * 1024
        ),
        cost_estimate=pl.CostEstimate(
            flops=flops, bytes_accessed=4 * 1024 * 1024, transcendentals=0
        ),
    )(facet_offsets, subgrid_offsets, facet_pixels, ct, st, rc, rs)
    return out.reshape(ib, 2, COLUMNS, mb)


def half_tables_rows(rows, half_i):
    r = np.arange(rows, dtype=np.int64)
    b = 2 * np.arange(half_i, dtype=np.int64) + 1
    t = (r[:, None] * b[None, :]) % (2 * IMAGE_N)
    angle = 2.0 * np.pi * t / (2 * IMAGE_N)
    return np.cos(angle), np.sin(angle)


def solution(mesh):
    in_specs = (P(None, "facet", "strip", None), P("facet", None), P())
    out_specs = P("strip", None, None, "facet")
    return jax.shard_map(
        per_device, mesh=mesh, in_specs=in_specs, out_specs=out_specs, check_vma=False
    )
```

```python
import functools
import math

import jax
import jax.numpy as jnp
import ml_dtypes
import numpy as np
from jax import lax
from jax.experimental import pallas as pl
from jax.experimental.pallas import tpu as pltpu
from jax.sharding import PartitionSpec as P

IMAGE_N = 65536
FREQ = 512
ROW_FREQ = 512
COLUMNS = 2
LANES = 128
CHUNK = 256
BF = jnp.bfloat16
F32 = jnp.float32
MESH = pl.DeviceIdType.MESH


def half_tables(count_a, count_b, step_a):
    a = 2 * np.arange(count_a, dtype=np.int64) + step_a
    b = 2 * np.arange(count_b, dtype=np.int64) + 1
    t = (a[:, None] * b[None, :]) % (4 * IMAGE_N)
    angle = 2.0 * np.pi * t / (4 * IMAGE_N)
    return np.cos(angle), np.sin(angle)


def cos_sin(product, modulus):
    t = (product + modulus // 2) & (modulus - 1)
    h = (t - modulus // 2).astype(F32) * (math.pi / modulus)
    h2 = h * h
    s = jnp.full_like(h, 1.0 / math.factorial(13))
    c = jnp.full_like(h, -1.0 / math.factorial(14))
    for n in range(11, 0, -2):
        s = s * h2 + (-1.0) ** ((n - 1) // 2) / math.factorial(n)
    for n in range(12, -1, -2):
        c = c * h2 + (-1.0) ** (n // 2) / math.factorial(n)
    s = s * h
    return 1.0 - 2.0 * s * s, 2.0 * s * c


def iota(shape, dim):
    return lax.broadcasted_iota(jnp.int32, shape, dim)


def dot(a, b):
    return jnp.dot(a, b, preferred_element_type=F32)


def kernel(
    facets, strips,
    fo_hbm, so_hbm, x_hbm, ct_hbm, st_hbm, rc_hbm, rs_hbm,
    out_ref,
    fo_ref, so_ref, x, ct, st, rc, rs, evod, ysend, yrecv, tc, ts, off_send, off_recv, zsend, zrecv,
    load_sem, y_ssem, y_rsem, o_ssem, o_rsem, z_ssem, z_rsem,
):
    f_me = lax.axis_index("facet")
    s_me = lax.axis_index("strip")
    rows, width = x.shape[1], x.shape[2]
    half_k = width // 2
    half_m = FREQ // 2
    half_i = ROW_FREQ // 2
    mb = FREQ // facets
    ib = ROW_FREQ // strips
    chunks = half_k // CHUNK
    scale = 1.0 / math.sqrt(width * rows * strips * facets)

    loads = []

    def load(src, dst):
        copy = pltpu.make_async_copy(src, dst, load_sem.at[len(loads)])
        copy.start()
        loads.append(copy)
        return copy

    fo_load = load(fo_hbm, fo_ref)
    so_load = load(so_hbm, so_ref)
    x_low, x_high = [], []
    for j in range(chunks):
        low = pl.ds((chunks - 1 - j) * CHUNK, CHUNK)
        high = pl.ds(half_k + j * CHUNK, CHUNK)
        x_low.append(load(x_hbm.at[:, 0, :, low], x.at[:, :, low]))
        x_high.append(load(x_hbm.at[:, 0, :, high], x.at[:, :, high]))
    ct_load = load(ct_hbm, ct)
    st_load = load(st_hbm, st)
    rc_load = load(rc_hbm, rc)
    rs_load = load(rs_hbm, rs)

    facet_peers = [lax.rem(f_me + d, facets) for d in range(1, facets)]
    strip_peers = [lax.rem(s_me + d, strips) for d in range(1, strips)]
    barrier = pltpu.get_barrier_semaphore()
    for peer in facet_peers:
        pl.semaphore_signal(barrier, inc=1, device_id=(peer, s_me), device_id_type=MESH)
    for peer in strip_peers:
        pl.semaphore_signal(barrier, inc=1, device_id=(f_me, peer), device_id_type=MESH)

    fo_load.wait()
    so_load.wait()
    fx = fo_ref[0, 0]
    fy = fo_ref[0, 1]
    u0 = [so_ref[c, 0] for c in range(COLUMNS)]
    w0 = [so_ref[c, 1] for c in range(COLUMNS)]

    off_send[...] = jnp.full(off_send.shape, fy, jnp.int32)
    off_recv[f_me] = off_send[...]

    pieces = half_k // LANES
    a_index = iota((pieces, LANES), 0) * LANES + iota((pieces, LANES), 1)
    pq = [
        cos_sin((2 * a_index + 1) * (2 * u0[c] + (FREQ - 1)), 4 * IMAGE_N)
        for c in range(COLUMNS)
    ]

    row = iota((8, half_m), 0)
    lane = iota((8, half_m), 1)
    first = jnp.where(row < 2, u0[0], u0[1])
    freq = first + jnp.where((row & 1) == 0, half_m + lane, half_m - 1 - lane)
    hc, hs = cos_sin((2 * fx + (width - 1)) * freq, 2 * IMAGE_N)
    hc, hs = hc * scale, hs * scale

    padded = -(-rows // LANES) * LANES
    row = iota((8, padded), 0)
    first = jnp.where(row == 0, w0[0], w0[1])
    pixel_row = s_me * rows + iota((8, padded), 1) + fy
    gc, gs = cos_sin((2 * first + (ROW_FREQ - 1)) * pixel_row, 2 * IMAGE_N)
    gc, gs = jnp.transpose(gc), jnp.transpose(gs)

    flip = (iota((CHUNK, CHUNK), 0) + iota((CHUNK, CHUNK), 1) == CHUNK - 1).astype(F32).astype(BF)

    def phase_column(c):
        for j in range(chunks):
            cols = pl.ds(j * CHUNK, CHUNK)
            if c == 0:
                x_low[j].wait()
                x_high[j].wait()
            low = x[:, :, pl.ds((chunks - 1 - j) * CHUNK, CHUNK)].reshape(2 * rows, CHUNK)
            high = x[:, :, pl.ds(half_k + j * CHUNK, CHUNK)].reshape(2 * rows, CHUNK).astype(F32)
            low = dot(low, flip)
            even = high + low
            odd = high - low
            er, ei, odr, odi = even[:rows], even[rows:], odd[:rows], odd[rows:]
            first = j * (CHUNK // LANES)
            p, q = (
                jnp.concatenate(
                    [part[first + n : first + n + 1] for n in range(CHUNK // LANES)], axis=1
                )
                for part in pq[c]
            )
            evod[c, 0, :rows, cols] = (er * p + odi * q).astype(BF)
            evod[c, 0, rows:, cols] = (ei * p - odr * q).astype(BF)
            evod[c, 1, :rows, cols] = (odr * p + ei * q).astype(BF)
            evod[c, 1, rows:, cols] = (odi * p - er * q).astype(BF)

    phase_column(0)
    pl.semaphore_wait(barrier, facets - 1 + strips - 1)

    def off_copy(d):
        return pltpu.make_async_remote_copy(
            src_ref=off_send,
            dst_ref=off_recv.at[f_me],
            send_sem=o_ssem.at[d - 1],
            recv_sem=o_rsem.at[d - 1],
            device_id=(facet_peers[d - 1], s_me),
            device_id_type=MESH,
        )

    def y_copy(c, d):
        return pltpu.make_async_remote_copy(
            src_ref=ysend.at[c, facet_peers[d - 1]],
            dst_ref=yrecv.at[c, f_me],
            send_sem=y_ssem.at[c, d - 1],
            recv_sem=y_rsem.at[c, d - 1],
            device_id=(facet_peers[d - 1], s_me),
            device_id_type=MESH,
        )

    def z_copy(c, d):
        return pltpu.make_async_remote_copy(
            src_ref=zsend.at[c, strip_peers[d - 1]],
            dst_ref=zrecv.at[c, d - 1],
            send_sem=z_ssem.at[c, d - 1],
            recv_sem=z_rsem.at[c, d - 1],
            device_id=(f_me, strip_peers[d - 1]),
            device_id_type=MESH,
        )

    off_copies = [off_copy(d) for d in range(1, facets)]
    for copy in off_copies:
        copy.start()

    y_copies = []
    for c in range(COLUMNS):
        if c > 0:
            phase_column(c)
        else:
            ct_load.wait()
            st_load.wait()
        pp = dot(evod[c, 0], ct[...])
        qq = dot(evod[c, 1], st[...])
        halves = []
        for sign in (0, 1):
            if sign == 0:
                yr = pp[:rows] + qq[rows:]
                yi = pp[rows:] - qq[:rows]
            else:
                yr = pp[:rows] - qq[rows:]
                yi = pp[rows:] + qq[:rows]
            hcr, hsr = hc[2 * c + sign : 2 * c + sign + 1], hs[2 * c + sign : 2 * c + sign + 1]
            gcr, gsr = gc[:rows, c : c + 1], gs[:rows, c : c + 1]
            a = gcr * hcr - gsr * hsr
            b = gcr * hsr + gsr * hcr
            halves.append(((yr * a + yi * b).astype(BF), (yi * a - yr * b).astype(BF)))
        for f in range(facets):
            if f >= facets // 2:
                yr, yi = halves[0]
                start = mb * f - half_m
            else:
                yr, yi = halves[1]
                start = half_m - mb * (f + 1)
            ysend[c, f] = jnp.concatenate(
                [yr[:, start : start + mb], yi[:, start : start + mb]], axis=1
            )
        copies = [y_copy(c, d) for d in range(1, facets)]
        for copy in copies:
            copy.start()
        y_copies.append(copies)
        yrecv[c, f_me] = ysend[c, f_me]

    for copy in off_copies:
        copy.wait_recv()
    rc_load.wait()
    rs_load.wait()
    offs = jnp.concatenate([off_recv[:, 0, :]] * (half_i // LANES), axis=1)
    phc, phs = cos_sin(
        (2 * iota((facets, half_i), 1) + 1) * (offs + s_me * rows), 2 * IMAGE_N
    )
    phc, phs = jnp.transpose(phc), jnp.transpose(phs)
    base_c, base_s = rc[...], rs[...]
    for f in range(facets):
        pc, ps = phc[:, f : f + 1], phs[:, f : f + 1]
        tc[:, f * rows : (f + 1) * rows] = (base_c * pc - base_s * ps).astype(BF)
        ts[:, f * rows : (f + 1) * rows] = (base_s * pc + base_c * ps).astype(BF)

    src, dst = iota((2 * mb, 2 * mb), 0), iota((2 * mb, 2 * mb), 1)
    same_part = (src >= mb) == (dst >= mb)
    mirrored = (src + dst - jnp.where(dst >= mb, 2 * mb, 0)) == mb - 1
    lower = jnp.where(f_me < facets // 2, 1, 0)
    picked = jnp.where(lower == 1, jnp.where(same_part & mirrored, 1, 0), jnp.where(src == dst, 1, 0))
    order = picked.astype(F32).astype(BF)

    z_copies = []
    for c in range(COLUMNS):
        for copy in y_copies[c]:
            copy.wait_recv()
        y = yrecv[c].reshape(facets * rows, 2 * mb)
        aa = dot(tc[...], y)
        bb = dot(ts[...], y)
        turned = jnp.concatenate([bb[:, mb:], -bb[:, :mb]], axis=1)
        upper_rows = dot((aa + turned).astype(BF), order).astype(BF)
        lower_rows = dot(flip, (aa - turned).astype(BF)).astype(BF)
        lower_rows = dot(lower_rows, order).astype(BF)
        z = jnp.concatenate([lower_rows, upper_rows], axis=0)
        zsend[c] = z.reshape(strips, ib, 2 * mb)
        copies = [z_copy(c, d) for d in range(1, strips)]
        for copy in copies:
            copy.start()
        z_copies.append(copies)

    totals = []
    for c in range(COLUMNS):
        total = zsend[c, s_me].astype(F32)
        for d in range(1, strips):
            z_copies[c][d - 1].wait_recv()
            total += zrecv[c, d - 1].astype(F32)
        totals.append(total)
    out_ref[...] = jnp.concatenate(
        [totals[0][:, :mb], totals[1][:, :mb], totals[0][:, mb:], totals[1][:, mb:]], axis=1
    )
    for copy in off_copies + y_copies[0] + y_copies[1] + z_copies[0] + z_copies[1]:
        copy.wait_send()


def per_device(facet_pixels, facet_offsets, subgrid_offsets):
    rows, width = facet_pixels.shape[2], facet_pixels.shape[3]
    facets, strips = lax.axis_size("facet"), lax.axis_size("strip")
    mb, ib = FREQ // facets, ROW_FREQ // strips
    half_k, half_m, half_i = width // 2, FREQ // 2, ROW_FREQ // 2
    ct, st = (t.astype(ml_dtypes.bfloat16) for t in half_tables(half_k, half_m, 1))
    rc, rs = (
        np.ascontiguousarray(t.T.astype(np.float32)) for t in half_tables_rows(rows, half_i)
    )
    loads = 2 * (half_k // CHUNK) + 6
    dma = pltpu.SemaphoreType.DMA
    flops = 2 * (4 * 2 * rows * half_k * half_m + 4 * half_i * facets * rows * 2 * mb)
    out = pl.pallas_call(
        functools.partial(kernel, facets, strips),
        out_shape=jax.ShapeDtypeStruct((ib, 4 * mb), F32),
        in_specs=[pl.BlockSpec(memory_space=pltpu.HBM)] * 7,
        out_specs=pl.BlockSpec(memory_space=pltpu.VMEM),
        scratch_shapes=[
            pltpu.SMEM((1, 2), jnp.int32),
            pltpu.SMEM((COLUMNS, 2), jnp.int32),
            pltpu.VMEM((2, rows, width), BF),
            pltpu.VMEM((half_k, half_m), BF),
            pltpu.VMEM((half_k, half_m), BF),
            pltpu.VMEM((half_i, rows), F32),
            pltpu.VMEM((half_i, rows), F32),
            pltpu.VMEM((COLUMNS, 2, 2 * rows, half_k), BF),
            pltpu.VMEM((COLUMNS, facets, rows, 2 * mb), BF),
            pltpu.VMEM((COLUMNS, facets, rows, 2 * mb), BF),
            pltpu.VMEM((half_i, facets * rows), BF),
            pltpu.VMEM((half_i, facets * rows), BF),
            pltpu.VMEM((8, LANES), jnp.int32),
            pltpu.VMEM((facets, 8, LANES), jnp.int32),
            pltpu.VMEM((COLUMNS, strips, ib, 2 * mb), BF),
            pltpu.VMEM((COLUMNS, strips - 1, ib, 2 * mb), BF),
            dma((loads,)),
            dma((COLUMNS, facets - 1)),
            dma((COLUMNS, facets - 1)),
            dma((facets - 1,)),
            dma((facets - 1,)),
            dma((COLUMNS, strips - 1)),
            dma((COLUMNS, strips - 1)),
        ],
        compiler_params=pltpu.CompilerParams(
            collective_id=0, has_side_effects=True, vmem_limit_bytes=40 * 1024 * 1024
        ),
        cost_estimate=pl.CostEstimate(
            flops=flops, bytes_accessed=4 * 1024 * 1024, transcendentals=0
        ),
    )(facet_offsets, subgrid_offsets, facet_pixels, ct, st, rc, rs)
    return out.reshape(ib, 2, COLUMNS, mb)


def half_tables_rows(rows, half_i):
    r = np.arange(rows, dtype=np.int64)
    b = 2 * np.arange(half_i, dtype=np.int64) + 1
    t = (r[:, None] * b[None, :]) % (2 * IMAGE_N)
    angle = 2.0 * np.pi * t / (2 * IMAGE_N)
    return np.cos(angle), np.sin(angle)


def solution(mesh):
    in_specs = (P(None, "facet", "strip", None), P("facet", None), P())
    out_specs = P("strip", None, None, "facet")
    return jax.shard_map(
        per_device, mesh=mesh, in_specs=in_specs, out_specs=out_specs, check_vma=False
    )
```

```python
import functools
import math

import jax
import jax.numpy as jnp
import ml_dtypes
import numpy as np
from jax import lax
from jax.experimental import pallas as pl
from jax.experimental.pallas import tpu as pltpu
from jax.sharding import PartitionSpec as P

IMAGE_N = 65536
FREQ = 512
ROW_FREQ = 512
COLUMNS = 2
LANES = 128
CHUNK = 256
BLOCK = 16
BF = jnp.bfloat16
F32 = jnp.float32
MESH = pl.DeviceIdType.MESH


def half_tables(count_a, count_b, step_a):
    a = 2 * np.arange(count_a, dtype=np.int64) + step_a
    b = 2 * np.arange(count_b, dtype=np.int64) + 1
    t = (a[:, None] * b[None, :]) % (4 * IMAGE_N)
    angle = 2.0 * np.pi * t / (4 * IMAGE_N)
    return np.cos(angle), np.sin(angle)


def cos_sin(product, modulus):
    t = (product + modulus // 2) & (modulus - 1)
    h = (t - modulus // 2).astype(F32) * (math.pi / modulus)
    h2 = h * h
    s = jnp.full_like(h, 1.0 / math.factorial(13))
    c = jnp.full_like(h, -1.0 / math.factorial(14))
    for n in range(11, 0, -2):
        s = s * h2 + (-1.0) ** ((n - 1) // 2) / math.factorial(n)
    for n in range(12, -1, -2):
        c = c * h2 + (-1.0) ** (n // 2) / math.factorial(n)
    s = s * h
    return 1.0 - 2.0 * s * s, 2.0 * s * c


def iota(shape, dim):
    return lax.broadcasted_iota(jnp.int32, shape, dim)


def dot(a, b):
    return jnp.dot(a, b, preferred_element_type=F32)


def kernel(
    facets, strips,
    fo_hbm, so_hbm, x_hbm, ct_hbm, st_hbm, rc_hbm, rs_hbm,
    out_ref,
    fo_ref, so_ref, x, xr, ct, st, rc, rs, evod, gc_ref, gs_ref, pp, qq, ysend, yrecv, tc, ts, off_send, off_recv, zsend, zrecv,
    load_sem, y_ssem, y_rsem, o_ssem, o_rsem, z_ssem, z_rsem,
):
    f_me = lax.axis_index("facet")
    s_me = lax.axis_index("strip")
    rows, width = x.shape[1], x.shape[2]
    half_k = width // 2
    half_m = FREQ // 2
    half_i = ROW_FREQ // 2
    mb = FREQ // facets
    ib = ROW_FREQ // strips
    chunks = half_k // CHUNK
    scale = 1.0 / math.sqrt(width * rows * strips * facets)

    loads = []

    def load(src, dst):
        copy = pltpu.make_async_copy(src, dst, load_sem.at[len(loads)])
        copy.start()
        loads.append(copy)
        return copy

    fo_load = load(fo_hbm, fo_ref)
    so_load = load(so_hbm, so_ref)
    x_low, x_high = [], []
    for j in range(chunks):
        low = pl.ds((chunks - 1 - j) * CHUNK, CHUNK)
        high = pl.ds(half_k + j * CHUNK, CHUNK)
        x_low.append(load(x_hbm.at[:, 0, :, low], x.at[:, :, low]))
        x_high.append(load(x_hbm.at[:, 0, :, high], x.at[:, :, high]))
    ct_load = load(ct_hbm, ct)
    st_load = load(st_hbm, st)
    rc_load = load(rc_hbm, rc)
    rs_load = load(rs_hbm, rs)

    facet_peers = [lax.rem(f_me + d, facets) for d in range(1, facets)]
    strip_peers = [lax.rem(s_me + d, strips) for d in range(1, strips)]
    barrier = pltpu.get_barrier_semaphore()
    for peer in facet_peers:
        pl.semaphore_signal(barrier, inc=1, device_id=(peer, s_me), device_id_type=MESH)
    for peer in strip_peers:
        pl.semaphore_signal(barrier, inc=1, device_id=(f_me, peer), device_id_type=MESH)

    fo_load.wait()
    so_load.wait()
    fx = fo_ref[0, 0]
    fy = fo_ref[0, 1]
    u0 = [so_ref[c, 0] for c in range(COLUMNS)]
    w0 = [so_ref[c, 1] for c in range(COLUMNS)]

    off_send[...] = jnp.full(off_send.shape, fy, jnp.int32)
    off_recv[f_me] = off_send[...]

    pieces = half_k // LANES
    a_index = iota((pieces, LANES), 0) * LANES + iota((pieces, LANES), 1)
    pq = [
        cos_sin((2 * a_index + 1) * (2 * u0[c] + (FREQ - 1)), 4 * IMAGE_N)
        for c in range(COLUMNS)
    ]

    row = iota((8, half_m), 0)
    lane = iota((8, half_m), 1)
    first = jnp.where(row < 2, u0[0], u0[1])
    freq = first + jnp.where((row & 1) == 0, half_m + lane, half_m - 1 - lane)
    hc, hs = cos_sin((2 * fx + (width - 1)) * freq, 2 * IMAGE_N)
    hc, hs = hc * scale, hs * scale

    padded = -(-rows // LANES) * LANES
    row = iota((8, padded), 0)
    first = jnp.where(row == 0, w0[0], w0[1])
    pixel_row = s_me * rows + iota((8, padded), 1) + fy
    gc, gs = cos_sin((2 * first + (ROW_FREQ - 1)) * pixel_row, 2 * IMAGE_N)
    gc_ref[...] = jnp.transpose(gc)
    gs_ref[...] = jnp.transpose(gs)

    flip = (iota((CHUNK, CHUNK), 0) + iota((CHUNK, CHUNK), 1) == CHUNK - 1).astype(F32).astype(BF)

    def row_block(n):
        return pl.ds(pl.multiple_of(n * BLOCK, BLOCK), BLOCK)

    def im_block(n):
        return pl.ds(pl.multiple_of(rows + n * BLOCK, BLOCK), BLOCK)

    def phase_column(c):
        for j in range(chunks):
            cols = pl.ds(j * CHUNK, CHUNK)
            high_cols = pl.ds(half_k + j * CHUNK, CHUNK)
            if c == 0:
                x_low[j].wait()
                x_high[j].wait()
                low = x[:, :, pl.ds((chunks - 1 - j) * CHUNK, CHUNK)].reshape(2 * rows, CHUNK)
                xr[:, cols] = dot(low, flip).astype(BF)
            first = j * (CHUNK // LANES)
            p, q = (
                jnp.concatenate(
                    [part[first + n : first + n + 1] for n in range(CHUNK // LANES)], axis=1
                )
                for part in pq[c]
            )

            def block(n, carry):
                re, im = row_block(n), im_block(n)
                hr, hi = x[0, re, high_cols].astype(F32), x[1, re, high_cols].astype(F32)
                lr, li = xr[re, cols].astype(F32), xr[im, cols].astype(F32)
                er, odr, ei, odi = hr + lr, hr - lr, hi + li, hi - li
                evod[c, 0, re, cols] = (er * p + odi * q).astype(BF)
                evod[c, 0, im, cols] = (ei * p - odr * q).astype(BF)
                evod[c, 1, re, cols] = (odr * p + ei * q).astype(BF)
                evod[c, 1, im, cols] = (odi * p - er * q).astype(BF)
                return carry

            lax.fori_loop(0, rows // BLOCK, block, 0, unroll=True)

    phase_column(0)
    pl.semaphore_wait(barrier, facets - 1 + strips - 1)

    def off_copy(d):
        return pltpu.make_async_remote_copy(
            src_ref=off_send,
            dst_ref=off_recv.at[f_me],
            send_sem=o_ssem.at[d - 1],
            recv_sem=o_rsem.at[d - 1],
            device_id=(facet_peers[d - 1], s_me),
            device_id_type=MESH,
        )

    def y_copy(c, d):
        return pltpu.make_async_remote_copy(
            src_ref=ysend.at[c, facet_peers[d - 1]],
            dst_ref=yrecv.at[c, f_me],
            send_sem=y_ssem.at[c, d - 1],
            recv_sem=y_rsem.at[c, d - 1],
            device_id=(facet_peers[d - 1], s_me),
            device_id_type=MESH,
        )

    def z_copy(c, d):
        return pltpu.make_async_remote_copy(
            src_ref=zsend.at[c, strip_peers[d - 1]],
            dst_ref=zrecv.at[c, d - 1],
            send_sem=z_ssem.at[c, d - 1],
            recv_sem=z_rsem.at[c, d - 1],
            device_id=(f_me, strip_peers[d - 1]),
            device_id_type=MESH,
        )

    off_copies = [off_copy(d) for d in range(1, facets)]
    for copy in off_copies:
        copy.start()

    y_copies = []
    for c in range(COLUMNS):
        if c > 0:
            phase_column(c)
        else:
            ct_load.wait()
            st_load.wait()
        pp[...] = dot(evod[c, 0], ct[...])
        qq[...] = dot(evod[c, 1], st[...])

        def block(n, carry):
            re, im = row_block(n), im_block(n)
            pr, pi, qr, qi = pp[re], pp[im], qq[re], qq[im]
            gcr, gsr = gc_ref[re, c : c + 1], gs_ref[re, c : c + 1]
            halves = []
            for sign, yr, yi in ((0, pr + qi, pi - qr), (1, pr - qi, pi + qr)):
                at = 2 * c + sign
                hcr, hsr = hc[at : at + 1], hs[at : at + 1]
                a = gcr * hcr - gsr * hsr
                b = gcr * hsr + gsr * hcr
                halves.append(((yr * a + yi * b).astype(BF), (yi * a - yr * b).astype(BF)))
            for f in range(facets):
                if f >= facets // 2:
                    yr, yi = halves[0]
                    start = mb * f - half_m
                else:
                    yr, yi = halves[1]
                    start = half_m - mb * (f + 1)
                ysend[c, f, re] = jnp.concatenate(
                    [yr[:, start : start + mb], yi[:, start : start + mb]], axis=1
                )
            return carry

        lax.fori_loop(0, rows // BLOCK, block, 0, unroll=True)
        copies = [y_copy(c, d) for d in range(1, facets)]
        for copy in copies:
            copy.start()
        y_copies.append(copies)
        yrecv[c, f_me] = ysend[c, f_me]

    for copy in off_copies:
        copy.wait_recv()
    rc_load.wait()
    rs_load.wait()
    offs = jnp.concatenate([off_recv[:, 0, :]] * (half_i // LANES), axis=1)
    phc, phs = cos_sin(
        (2 * iota((facets, half_i), 1) + 1) * (offs + s_me * rows), 2 * IMAGE_N
    )
    phc, phs = jnp.transpose(phc), jnp.transpose(phs)
    base_c, base_s = rc[...], rs[...]
    for f in range(facets):
        pc, ps = phc[:, f : f + 1], phs[:, f : f + 1]
        tc[:, f * rows : (f + 1) * rows] = (base_c * pc - base_s * ps).astype(BF)
        ts[:, f * rows : (f + 1) * rows] = (base_s * pc + base_c * ps).astype(BF)

    src, dst = iota((2 * mb, 2 * mb), 0), iota((2 * mb, 2 * mb), 1)
    same_part = (src >= mb) == (dst >= mb)
    mirrored = (src + dst - jnp.where(dst >= mb, 2 * mb, 0)) == mb - 1
    lower = jnp.where(f_me < facets // 2, 1, 0)
    picked = jnp.where(lower == 1, jnp.where(same_part & mirrored, 1, 0), jnp.where(src == dst, 1, 0))
    order = picked.astype(F32).astype(BF)

    z_copies = []
    for c in range(COLUMNS):
        for copy in y_copies[c]:
            copy.wait_recv()
        y = yrecv[c].reshape(facets * rows, 2 * mb)
        aa = dot(tc[...], y)
        bb = dot(ts[...], y)
        turned = jnp.concatenate([bb[:, mb:], -bb[:, :mb]], axis=1)
        upper_rows = dot((aa + turned).astype(BF), order).astype(BF)
        lower_rows = dot(flip, (aa - turned).astype(BF)).astype(BF)
        lower_rows = dot(lower_rows, order).astype(BF)
        z = jnp.concatenate([lower_rows, upper_rows], axis=0)
        zsend[c] = z.reshape(strips, ib, 2 * mb)
        copies = [z_copy(c, d) for d in range(1, strips)]
        for copy in copies:
            copy.start()
        z_copies.append(copies)

    totals = []
    for c in range(COLUMNS):
        total = zsend[c, s_me].astype(F32)
        for d in range(1, strips):
            z_copies[c][d - 1].wait_recv()
            total += zrecv[c, d - 1].astype(F32)
        totals.append(total)
    out_ref[...] = jnp.transpose(
        jnp.concatenate(
            [totals[0][:, :mb], totals[1][:, :mb], totals[0][:, mb:], totals[1][:, mb:]], axis=1
        )
    )
    for copy in off_copies + y_copies[0] + y_copies[1] + z_copies[0] + z_copies[1]:
        copy.wait_send()


def per_device(facet_pixels, facet_offsets, subgrid_offsets):
    rows, width = facet_pixels.shape[2], facet_pixels.shape[3]
    facets, strips = lax.axis_size("facet"), lax.axis_size("strip")
    mb, ib = FREQ // facets, ROW_FREQ // strips
    half_k, half_m, half_i = width // 2, FREQ // 2, ROW_FREQ // 2
    ct, st = (t.astype(ml_dtypes.bfloat16) for t in half_tables(half_k, half_m, 1))
    rc, rs = (
        np.ascontiguousarray(t.T.astype(np.float32)) for t in half_tables_rows(rows, half_i)
    )
    padded = -(-rows // LANES) * LANES
    loads = 2 * (half_k // CHUNK) + 6
    dma = pltpu.SemaphoreType.DMA
    flops = 2 * (4 * 2 * rows * half_k * half_m + 4 * half_i * facets * rows * 2 * mb)
    out = pl.pallas_call(
        functools.partial(kernel, facets, strips),
        out_shape=jax.ShapeDtypeStruct((4 * mb, ib), F32),
        in_specs=[pl.BlockSpec(memory_space=pltpu.HBM)] * 7,
        out_specs=pl.BlockSpec(memory_space=pltpu.VMEM),
        scratch_shapes=[
            pltpu.SMEM((1, 2), jnp.int32),
            pltpu.SMEM((COLUMNS, 2), jnp.int32),
            pltpu.VMEM((2, rows, width), BF),
            pltpu.VMEM((2 * rows, half_k), BF),
            pltpu.VMEM((half_k, half_m), BF),
            pltpu.VMEM((half_k, half_m), BF),
            pltpu.VMEM((half_i, rows), F32),
            pltpu.VMEM((half_i, rows), F32),
            pltpu.VMEM((COLUMNS, 2, 2 * rows, half_k), BF),
            pltpu.VMEM((padded, 8), F32),
            pltpu.VMEM((padded, 8), F32),
            pltpu.VMEM((2 * rows, half_m), F32),
            pltpu.VMEM((2 * rows, half_m), F32),
            pltpu.VMEM((COLUMNS, facets, rows, 2 * mb), BF),
            pltpu.VMEM((COLUMNS, facets, rows, 2 * mb), BF),
            pltpu.VMEM((half_i, facets * rows), BF),
            pltpu.VMEM((half_i, facets * rows), BF),
            pltpu.VMEM((8, LANES), jnp.int32),
            pltpu.VMEM((facets, 8, LANES), jnp.int32),
            pltpu.VMEM((COLUMNS, strips, ib, 2 * mb), BF),
            pltpu.VMEM((COLUMNS, strips - 1, ib, 2 * mb), BF),
            dma((loads,)),
            dma((COLUMNS, facets - 1)),
            dma((COLUMNS, facets - 1)),
            dma((facets - 1,)),
            dma((facets - 1,)),
            dma((COLUMNS, strips - 1)),
            dma((COLUMNS, strips - 1)),
        ],
        compiler_params=pltpu.CompilerParams(
            collective_id=0, has_side_effects=True, vmem_limit_bytes=63 * 1024 * 1024
        ),
        cost_estimate=pl.CostEstimate(
            flops=flops, bytes_accessed=4 * 1024 * 1024, transcendentals=0
        ),
    )(facet_offsets, subgrid_offsets, facet_pixels, ct, st, rc, rs)
    return jnp.transpose(out.reshape(2, COLUMNS, mb, ib), (3, 0, 1, 2))


def half_tables_rows(rows, half_i):
    r = np.arange(rows, dtype=np.int64)
    b = 2 * np.arange(half_i, dtype=np.int64) + 1
    t = (r[:, None] * b[None, :]) % (2 * IMAGE_N)
    angle = 2.0 * np.pi * t / (2 * IMAGE_N)
    return np.cos(angle), np.sin(angle)


def solution(mesh):
    in_specs = (P(None, "facet", "strip", None), P("facet", None), P())
    out_specs = P("strip", None, None, "facet")
    return jax.shard_map(
        per_device, mesh=mesh, in_specs=in_specs, out_specs=out_specs, check_vma=False
    )
```

```python
import functools
import math

import jax
import jax.numpy as jnp
import ml_dtypes
import numpy as np
from jax import lax
from jax.experimental import pallas as pl
from jax.experimental.pallas import tpu as pltpu
from jax.sharding import PartitionSpec as P

IMAGE_N = 65536
FREQ = 512
ROW_FREQ = 512
COLUMNS = 2
LANES = 128
CHUNK = 256
BLOCK = 16
GROUPS = 2
BF = jnp.bfloat16
F32 = jnp.float32
MESH = pl.DeviceIdType.MESH


def half_tables(count_a, count_b, step_a):
    a = 2 * np.arange(count_a, dtype=np.int64) + step_a
    b = 2 * np.arange(count_b, dtype=np.int64) + 1
    t = (a[:, None] * b[None, :]) % (4 * IMAGE_N)
    angle = 2.0 * np.pi * t / (4 * IMAGE_N)
    return np.cos(angle), np.sin(angle)


def cos_sin(product, modulus):
    t = (product + modulus // 2) & (modulus - 1)
    h = (t - modulus // 2).astype(F32) * (math.pi / modulus)
    h2 = h * h
    s = jnp.full_like(h, 1.0 / math.factorial(13))
    c = jnp.full_like(h, -1.0 / math.factorial(14))
    for n in range(11, 0, -2):
        s = s * h2 + (-1.0) ** ((n - 1) // 2) / math.factorial(n)
    for n in range(12, -1, -2):
        c = c * h2 + (-1.0) ** (n // 2) / math.factorial(n)
    s = s * h
    return 1.0 - 2.0 * s * s, 2.0 * s * c


def iota(shape, dim):
    return lax.broadcasted_iota(jnp.int32, shape, dim)


def dot(a, b):
    return jnp.dot(a, b, preferred_element_type=F32)


def kernel(
    facets, strips,
    fo_hbm, so_hbm, x_hbm, ct_hbm, st_hbm, rc_hbm, rs_hbm,
    out_ref,
    fo_ref, so_ref, x, xr, ct, st, rc, rs, evod, gc_ref, gs_ref, pp, qq, ysend, yrecv, tc, ts, off_send, off_recv, zsend, zrecv,
    load_sem, y_ssem, y_rsem, o_ssem, o_rsem, z_ssem, z_rsem,
):
    f_me = lax.axis_index("facet")
    s_me = lax.axis_index("strip")
    rows, width = x.shape[1], x.shape[2]
    half_k = width // 2
    half_m = FREQ // 2
    half_i = ROW_FREQ // 2
    mb = FREQ // facets
    ib = ROW_FREQ // strips
    chunks = half_k // CHUNK
    scale = 1.0 / math.sqrt(width * rows * strips * facets)

    loads = []

    def load(src, dst):
        copy = pltpu.make_async_copy(src, dst, load_sem.at[len(loads)])
        copy.start()
        loads.append(copy)
        return copy

    fo_load = load(fo_hbm, fo_ref)
    so_load = load(so_hbm, so_ref)
    x_low, x_high, ct_load, st_load = [], [], [], []
    for g in range(GROUPS):
        for j in range(g * chunks // GROUPS, (g + 1) * chunks // GROUPS):
            low = pl.ds((chunks - 1 - j) * CHUNK, CHUNK)
            high = pl.ds(half_k + j * CHUNK, CHUNK)
            x_low.append(load(x_hbm.at[:, 0, :, low], x.at[:, :, low]))
            x_high.append(load(x_hbm.at[:, 0, :, high], x.at[:, :, high]))
        span = pl.ds(g * half_k // GROUPS, half_k // GROUPS)
        ct_load.append(load(ct_hbm.at[span], ct.at[span]))
        st_load.append(load(st_hbm.at[span], st.at[span]))
    rc_load = load(rc_hbm, rc)
    rs_load = load(rs_hbm, rs)

    facet_peers = [lax.rem(f_me + d, facets) for d in range(1, facets)]
    strip_peers = [lax.rem(s_me + d, strips) for d in range(1, strips)]
    barrier = pltpu.get_barrier_semaphore()
    for peer in facet_peers:
        pl.semaphore_signal(barrier, inc=1, device_id=(peer, s_me), device_id_type=MESH)
    for peer in strip_peers:
        pl.semaphore_signal(barrier, inc=1, device_id=(f_me, peer), device_id_type=MESH)

    fo_load.wait()
    so_load.wait()
    fx = fo_ref[0, 0]
    fy = fo_ref[0, 1]
    u0 = [so_ref[c, 0] for c in range(COLUMNS)]
    w0 = [so_ref[c, 1] for c in range(COLUMNS)]

    off_send[...] = jnp.full(off_send.shape, fy, jnp.int32)
    off_recv[f_me] = off_send[...]

    pieces = half_k // LANES
    a_index = iota((pieces, LANES), 0) * LANES + iota((pieces, LANES), 1)
    pq = [
        cos_sin((2 * a_index + 1) * (2 * u0[c] + (FREQ - 1)), 4 * IMAGE_N)
        for c in range(COLUMNS)
    ]

    row = iota((8, half_m), 0)
    lane = iota((8, half_m), 1)
    first = jnp.where(row < 2, u0[0], u0[1])
    freq = first + jnp.where((row & 1) == 0, half_m + lane, half_m - 1 - lane)
    hc, hs = cos_sin((2 * fx + (width - 1)) * freq, 2 * IMAGE_N)
    hc, hs = hc * scale, hs * scale

    padded = -(-rows // LANES) * LANES
    row = iota((8, padded), 0)
    first = jnp.where(row == 0, w0[0], w0[1])
    pixel_row = s_me * rows + iota((8, padded), 1) + fy
    gc, gs = cos_sin((2 * first + (ROW_FREQ - 1)) * pixel_row, 2 * IMAGE_N)
    gc_ref[...] = jnp.transpose(gc)
    gs_ref[...] = jnp.transpose(gs)

    flip = (iota((CHUNK, CHUNK), 0) + iota((CHUNK, CHUNK), 1) == CHUNK - 1).astype(F32).astype(BF)

    def row_block(n):
        return pl.ds(pl.multiple_of(n * BLOCK, BLOCK), BLOCK)

    def im_block(n):
        return pl.ds(pl.multiple_of(rows + n * BLOCK, BLOCK), BLOCK)

    def column_products(c):
        per_group = chunks // GROUPS
        for g in range(GROUPS):
            group = range(g * per_group, (g + 1) * per_group)
            span = pl.ds(g * per_group * CHUNK, per_group * CHUNK)
            if c == 0:
                for j in group:
                    x_low[j].wait()
                    x_high[j].wait()
                for j in group:
                    low = x[:, :, pl.ds((chunks - 1 - j) * CHUNK, CHUNK)].reshape(2 * rows, CHUNK)
                    xr[:, pl.ds(j * CHUNK, CHUNK)] = dot(low, flip).astype(BF)
            for j in group:
                phase_chunk(c, j)
            if c == 0:
                ct_load[g].wait()
                st_load[g].wait()
            p_part = dot(evod[c, 0, :, span], ct[span])
            q_part = dot(evod[c, 1, :, span], st[span])
            pp[c] = p_part if g == 0 else pp[c] + p_part
            qq[c] = q_part if g == 0 else qq[c] + q_part

    def phase_chunk(c, j):
        cols = pl.ds(j * CHUNK, CHUNK)
        high_cols = pl.ds(half_k + j * CHUNK, CHUNK)
        first = j * (CHUNK // LANES)
        p, q = (
            jnp.concatenate(
                [part[first + n : first + n + 1] for n in range(CHUNK // LANES)], axis=1
            )
            for part in pq[c]
        )

        def block(n, carry):
            re, im = row_block(n), im_block(n)
            hr, hi = x[0, re, high_cols].astype(F32), x[1, re, high_cols].astype(F32)
            lr, li = xr[re, cols].astype(F32), xr[im, cols].astype(F32)
            er, odr, ei, odi = hr + lr, hr - lr, hi + li, hi - li
            evod[c, 0, re, cols] = (er * p + odi * q).astype(BF)
            evod[c, 0, im, cols] = (ei * p - odr * q).astype(BF)
            evod[c, 1, re, cols] = (odr * p + ei * q).astype(BF)
            evod[c, 1, im, cols] = (odi * p - er * q).astype(BF)
            return carry

        lax.fori_loop(0, rows // BLOCK, block, 0, unroll=True)

    column_products(0)
    pl.semaphore_wait(barrier, facets - 1 + strips - 1)

    def off_copy(d):
        return pltpu.make_async_remote_copy(
            src_ref=off_send,
            dst_ref=off_recv.at[f_me],
            send_sem=o_ssem.at[d - 1],
            recv_sem=o_rsem.at[d - 1],
            device_id=(facet_peers[d - 1], s_me),
            device_id_type=MESH,
        )

    def y_copy(c, d):
        return pltpu.make_async_remote_copy(
            src_ref=ysend.at[c, facet_peers[d - 1]],
            dst_ref=yrecv.at[c, f_me],
            send_sem=y_ssem.at[c, d - 1],
            recv_sem=y_rsem.at[c, d - 1],
            device_id=(facet_peers[d - 1], s_me),
            device_id_type=MESH,
        )

    def z_copy(c, d):
        return pltpu.make_async_remote_copy(
            src_ref=zsend.at[c, strip_peers[d - 1]],
            dst_ref=zrecv.at[c, d - 1],
            send_sem=z_ssem.at[c, d - 1],
            recv_sem=z_rsem.at[c, d - 1],
            device_id=(f_me, strip_peers[d - 1]),
            device_id_type=MESH,
        )

    off_copies = [off_copy(d) for d in range(1, facets)]
    for copy in off_copies:
        copy.start()

    y_copies = []
    for c in range(COLUMNS):
        if c > 0:
            column_products(c)

        def block(n, carry):
            re, im = row_block(n), im_block(n)
            pr, pi, qr, qi = pp[c, re], pp[c, im], qq[c, re], qq[c, im]
            gcr, gsr = gc_ref[re, c : c + 1], gs_ref[re, c : c + 1]
            halves = []
            for sign, yr, yi in ((0, pr + qi, pi - qr), (1, pr - qi, pi + qr)):
                at = 2 * c + sign
                hcr, hsr = hc[at : at + 1], hs[at : at + 1]
                a = gcr * hcr - gsr * hsr
                b = gcr * hsr + gsr * hcr
                halves.append(((yr * a + yi * b).astype(BF), (yi * a - yr * b).astype(BF)))
            for f in range(facets):
                if f >= facets // 2:
                    yr, yi = halves[0]
                    start = mb * f - half_m
                else:
                    yr, yi = halves[1]
                    start = half_m - mb * (f + 1)
                ysend[c, f, re] = jnp.concatenate(
                    [yr[:, start : start + mb], yi[:, start : start + mb]], axis=1
                )
            return carry

        lax.fori_loop(0, rows // BLOCK, block, 0, unroll=True)
        copies = [y_copy(c, d) for d in range(1, facets)]
        for copy in copies:
            copy.start()
        y_copies.append(copies)
        yrecv[c, f_me] = ysend[c, f_me]

    for copy in off_copies:
        copy.wait_recv()
    rc_load.wait()
    rs_load.wait()
    offs = jnp.concatenate([off_recv[:, 0, :]] * (half_i // LANES), axis=1)
    phc, phs = cos_sin(
        (2 * iota((facets, half_i), 1) + 1) * (offs + s_me * rows), 2 * IMAGE_N
    )
    phc, phs = jnp.transpose(phc), jnp.transpose(phs)
    base_c, base_s = rc[...], rs[...]
    for f in range(facets):
        pc, ps = phc[:, f : f + 1], phs[:, f : f + 1]
        tc[:, f * rows : (f + 1) * rows] = (base_c * pc - base_s * ps).astype(BF)
        ts[:, f * rows : (f + 1) * rows] = (base_s * pc + base_c * ps).astype(BF)

    src, dst = iota((2 * mb, 2 * mb), 0), iota((2 * mb, 2 * mb), 1)
    same_part = (src >= mb) == (dst >= mb)
    mirrored = (src + dst - jnp.where(dst >= mb, 2 * mb, 0)) == mb - 1
    lower = jnp.where(f_me < facets // 2, 1, 0)
    picked = jnp.where(lower == 1, jnp.where(same_part & mirrored, 1, 0), jnp.where(src == dst, 1, 0))
    order = picked.astype(F32).astype(BF)

    z_copies = []
    for c in range(COLUMNS):
        for copy in y_copies[c]:
            copy.wait_recv()
        y = yrecv[c].reshape(facets * rows, 2 * mb)
        aa = dot(tc[...], y)
        bb = dot(ts[...], y)
        turned = jnp.concatenate([bb[:, mb:], -bb[:, :mb]], axis=1)
        upper_rows = dot((aa + turned).astype(BF), order).astype(BF)
        lower_rows = dot(flip, (aa - turned).astype(BF)).astype(BF)
        lower_rows = dot(lower_rows, order).astype(BF)
        z = jnp.concatenate([lower_rows, upper_rows], axis=0)
        zsend[c] = z.reshape(strips, ib, 2 * mb)
        copies = [z_copy(c, d) for d in range(1, strips)]
        for copy in copies:
            copy.start()
        z_copies.append(copies)

    totals = []
    for c in range(COLUMNS):
        total = zsend[c, s_me].astype(F32)
        for d in range(1, strips):
            z_copies[c][d - 1].wait_recv()
            total += zrecv[c, d - 1].astype(F32)
        totals.append(total)
    out_ref[...] = jnp.transpose(
        jnp.concatenate(
            [totals[0][:, :mb], totals[1][:, :mb], totals[0][:, mb:], totals[1][:, mb:]], axis=1
        )
    )
    for copy in off_copies + y_copies[0] + y_copies[1] + z_copies[0] + z_copies[1]:
        copy.wait_send()


def per_device(facet_pixels, facet_offsets, subgrid_offsets):
    rows, width = facet_pixels.shape[2], facet_pixels.shape[3]
    facets, strips = lax.axis_size("facet"), lax.axis_size("strip")
    mb, ib = FREQ // facets, ROW_FREQ // strips
    half_k, half_m, half_i = width // 2, FREQ // 2, ROW_FREQ // 2
    ct, st = (t.astype(ml_dtypes.bfloat16) for t in half_tables(half_k, half_m, 1))
    rc, rs = (
        np.ascontiguousarray(t.T.astype(np.float32)) for t in half_tables_rows(rows, half_i)
    )
    padded = -(-rows // LANES) * LANES
    loads = 2 * (half_k // CHUNK) + 2 * GROUPS + 4
    dma = pltpu.SemaphoreType.DMA
    flops = 2 * (4 * 2 * rows * half_k * half_m + 4 * half_i * facets * rows * 2 * mb)
    out = pl.pallas_call(
        functools.partial(kernel, facets, strips),
        out_shape=jax.ShapeDtypeStruct((4 * mb, ib), F32),
        in_specs=[pl.BlockSpec(memory_space=pltpu.HBM)] * 7,
        out_specs=pl.BlockSpec(memory_space=pltpu.VMEM),
        scratch_shapes=[
            pltpu.SMEM((1, 2), jnp.int32),
            pltpu.SMEM((COLUMNS, 2), jnp.int32),
            pltpu.VMEM((2, rows, width), BF),
            pltpu.VMEM((2 * rows, half_k), BF),
            pltpu.VMEM((half_k, half_m), BF),
            pltpu.VMEM((half_k, half_m), BF),
            pltpu.VMEM((half_i, rows), F32),
            pltpu.VMEM((half_i, rows), F32),
            pltpu.VMEM((COLUMNS, 2, 2 * rows, half_k), BF),
            pltpu.VMEM((padded, 8), F32),
            pltpu.VMEM((padded, 8), F32),
            pltpu.VMEM((COLUMNS, 2 * rows, half_m), F32),
            pltpu.VMEM((COLUMNS, 2 * rows, half_m), F32),
            pltpu.VMEM((COLUMNS, facets, rows, 2 * mb), BF),
            pltpu.VMEM((COLUMNS, facets, rows, 2 * mb), BF),
            pltpu.VMEM((half_i, facets * rows), BF),
            pltpu.VMEM((half_i, facets * rows), BF),
            pltpu.VMEM((8, LANES), jnp.int32),
            pltpu.VMEM((facets, 8, LANES), jnp.int32),
            pltpu.VMEM((COLUMNS, strips, ib, 2 * mb), BF),
            pltpu.VMEM((COLUMNS, strips - 1, ib, 2 * mb), BF),
            dma((loads,)),
            dma((COLUMNS, facets - 1)),
            dma((COLUMNS, facets - 1)),
            dma((facets - 1,)),
            dma((facets - 1,)),
            dma((COLUMNS, strips - 1)),
            dma((COLUMNS, strips - 1)),
        ],
        compiler_params=pltpu.CompilerParams(
            collective_id=0, has_side_effects=True, vmem_limit_bytes=63 * 1024 * 1024
        ),
        cost_estimate=pl.CostEstimate(
            flops=flops, bytes_accessed=4 * 1024 * 1024, transcendentals=0
        ),
    )(facet_offsets, subgrid_offsets, facet_pixels, ct, st, rc, rs)
    return jnp.transpose(out.reshape(2, COLUMNS, mb, ib), (3, 0, 1, 2))


def half_tables_rows(rows, half_i):
    r = np.arange(rows, dtype=np.int64)
    b = 2 * np.arange(half_i, dtype=np.int64) + 1
    t = (r[:, None] * b[None, :]) % (2 * IMAGE_N)
    angle = 2.0 * np.pi * t / (2 * IMAGE_N)
    return np.cos(angle), np.sin(angle)


def solution(mesh):
    in_specs = (P(None, "facet", "strip", None), P("facet", None), P())
    out_specs = P("strip", None, None, "facet")
    return jax.shard_map(
        per_device, mesh=mesh, in_specs=in_specs, out_specs=out_specs, check_vma=False
    )
```

```python
import functools
import math

import jax
import jax.numpy as jnp
import ml_dtypes
import numpy as np
from jax import lax
from jax.experimental import pallas as pl
from jax.experimental.pallas import tpu as pltpu
from jax.sharding import PartitionSpec as P

IMAGE_N = 65536
FREQ = 512
ROW_FREQ = 512
COLUMNS = 2
LANES = 128
CHUNK = 256
BLOCK = 16
GROUPS = 2
BF = jnp.bfloat16
F32 = jnp.float32
MESH = pl.DeviceIdType.MESH


def half_tables(count_a, count_b, step_a):
    a = 2 * np.arange(count_a, dtype=np.int64) + step_a
    b = 2 * np.arange(count_b, dtype=np.int64) + 1
    t = (a[:, None] * b[None, :]) % (4 * IMAGE_N)
    angle = 2.0 * np.pi * t / (4 * IMAGE_N)
    return np.cos(angle), np.sin(angle)


def cos_sin(product, modulus):
    t = (product + modulus // 2) & (modulus - 1)
    h = (t - modulus // 2).astype(F32) * (math.pi / modulus)
    h2 = h * h
    s = jnp.full_like(h, 1.0 / math.factorial(13))
    c = jnp.full_like(h, -1.0 / math.factorial(14))
    for n in range(11, 0, -2):
        s = s * h2 + (-1.0) ** ((n - 1) // 2) / math.factorial(n)
    for n in range(12, -1, -2):
        c = c * h2 + (-1.0) ** (n // 2) / math.factorial(n)
    s = s * h
    return 1.0 - 2.0 * s * s, 2.0 * s * c


def partner(me, d, count):
    peer, bit = 0, 1
    while bit < count:
        digit = me // bit % 2
        peer = peer + bit * ((1 - digit) if d & bit else digit)
        bit *= 2
    return peer


def spread_order(count):
    quarter = count // 4
    order = []
    for n in range(quarter):
        order += [3 * quarter + n, 2 * quarter + n]
    return order + [d for d in range(2 * quarter - 1, 0, -1)]


def iota(shape, dim):
    return lax.broadcasted_iota(jnp.int32, shape, dim)


def dot(a, b):
    return jnp.dot(a, b, preferred_element_type=F32)


def kernel(
    facets, strips,
    fo_hbm, so_hbm, x_hbm, ct_hbm, st_hbm, rc_hbm, rs_hbm,
    out_ref,
    fo_ref, so_ref, x, xr, ct, st, rc, rs, evod, gc_ref, gs_ref, pp, qq, ysend, yrecv, tc, ts, off_send, off_recv, zsend, zrecv,
    load_sem, y_ssem, y_rsem, o_ssem, o_rsem, z_ssem, z_rsem,
):
    f_me = lax.axis_index("facet")
    s_me = lax.axis_index("strip")
    rows, width = x.shape[1], x.shape[2]
    half_k = width // 2
    half_m = FREQ // 2
    half_i = ROW_FREQ // 2
    mb = FREQ // facets
    ib = ROW_FREQ // strips
    chunks = half_k // CHUNK
    scale = 1.0 / math.sqrt(width * rows * strips * facets)

    loads = []

    def load(src, dst):
        copy = pltpu.make_async_copy(src, dst, load_sem.at[len(loads)])
        copy.start()
        loads.append(copy)
        return copy

    fo_load = load(fo_hbm, fo_ref)
    so_load = load(so_hbm, so_ref)
    x_low, x_high, ct_load, st_load = [], [], [], []
    for g in range(GROUPS):
        for j in range(g * chunks // GROUPS, (g + 1) * chunks // GROUPS):
            low = pl.ds((chunks - 1 - j) * CHUNK, CHUNK)
            high = pl.ds(half_k + j * CHUNK, CHUNK)
            x_low.append(load(x_hbm.at[:, 0, :, low], x.at[:, :, low]))
            x_high.append(load(x_hbm.at[:, 0, :, high], x.at[:, :, high]))
        span = pl.ds(g * half_k // GROUPS, half_k // GROUPS)
        ct_load.append(load(ct_hbm.at[span], ct.at[span]))
        st_load.append(load(st_hbm.at[span], st.at[span]))
    rc_load = load(rc_hbm, rc)
    rs_load = load(rs_hbm, rs)

    facet_peers = [partner(f_me, d, facets) for d in range(1, facets)]
    strip_peers = [partner(s_me, d, strips) for d in range(1, strips)]
    barrier = pltpu.get_barrier_semaphore()
    for peer in facet_peers:
        pl.semaphore_signal(barrier, inc=1, device_id=(peer, s_me), device_id_type=MESH)
    for peer in strip_peers:
        pl.semaphore_signal(barrier, inc=1, device_id=(f_me, peer), device_id_type=MESH)

    fo_load.wait()
    so_load.wait()
    fx = fo_ref[0, 0]
    fy = fo_ref[0, 1]
    u0 = [so_ref[c, 0] for c in range(COLUMNS)]
    w0 = [so_ref[c, 1] for c in range(COLUMNS)]

    off_send[...] = jnp.full(off_send.shape, fy, jnp.int32)
    off_recv[f_me] = off_send[...]

    pieces = half_k // LANES
    a_index = iota((pieces, LANES), 0) * LANES + iota((pieces, LANES), 1)
    pq = [
        cos_sin((2 * a_index + 1) * (2 * u0[c] + (FREQ - 1)), 4 * IMAGE_N)
        for c in range(COLUMNS)
    ]

    row = iota((8, half_m), 0)
    lane = iota((8, half_m), 1)
    first = jnp.where(row < 2, u0[0], u0[1])
    freq = first + jnp.where((row & 1) == 0, half_m + lane, half_m - 1 - lane)
    hc, hs = cos_sin((2 * fx + (width - 1)) * freq, 2 * IMAGE_N)
    hc, hs = hc * scale, hs * scale

    padded = -(-rows // LANES) * LANES
    row = iota((8, padded), 0)
    first = jnp.where(row == 0, w0[0], w0[1])
    pixel_row = s_me * rows + iota((8, padded), 1) + fy
    gc, gs = cos_sin((2 * first + (ROW_FREQ - 1)) * pixel_row, 2 * IMAGE_N)
    gc_ref[...] = jnp.transpose(gc)
    gs_ref[...] = jnp.transpose(gs)

    flip = (iota((CHUNK, CHUNK), 0) + iota((CHUNK, CHUNK), 1) == CHUNK - 1).astype(F32).astype(BF)

    def row_block(n):
        return pl.ds(pl.multiple_of(n * BLOCK, BLOCK), BLOCK)

    def im_block(n):
        return pl.ds(pl.multiple_of(rows + n * BLOCK, BLOCK), BLOCK)

    def column_products(c):
        per_group = chunks // GROUPS
        for g in range(GROUPS):
            group = range(g * per_group, (g + 1) * per_group)
            span = pl.ds(g * per_group * CHUNK, per_group * CHUNK)
            if c == 0:
                for j in group:
                    x_low[j].wait()
                    x_high[j].wait()
                for j in group:
                    low = x[:, :, pl.ds((chunks - 1 - j) * CHUNK, CHUNK)].reshape(2 * rows, CHUNK)
                    xr[:, pl.ds(j * CHUNK, CHUNK)] = dot(low, flip).astype(BF)
            for j in group:
                phase_chunk(c, j)
            if c == 0:
                ct_load[g].wait()
                st_load[g].wait()
            p_part = dot(evod[c, 0, :, span], ct[span])
            q_part = dot(evod[c, 1, :, span], st[span])
            pp[c] = p_part if g == 0 else pp[c] + p_part
            qq[c] = q_part if g == 0 else qq[c] + q_part

    def phase_chunk(c, j):
        cols = pl.ds(j * CHUNK, CHUNK)
        high_cols = pl.ds(half_k + j * CHUNK, CHUNK)
        first = j * (CHUNK // LANES)
        p, q = (
            jnp.concatenate(
                [part[first + n : first + n + 1] for n in range(CHUNK // LANES)], axis=1
            )
            for part in pq[c]
        )

        def block(n, carry):
            re, im = row_block(n), im_block(n)
            hr, hi = x[0, re, high_cols].astype(F32), x[1, re, high_cols].astype(F32)
            lr, li = xr[re, cols].astype(F32), xr[im, cols].astype(F32)
            er, odr, ei, odi = hr + lr, hr - lr, hi + li, hi - li
            evod[c, 0, re, cols] = (er * p + odi * q).astype(BF)
            evod[c, 0, im, cols] = (ei * p - odr * q).astype(BF)
            evod[c, 1, re, cols] = (odr * p + ei * q).astype(BF)
            evod[c, 1, im, cols] = (odi * p - er * q).astype(BF)
            return carry

        lax.fori_loop(0, rows // BLOCK, block, 0, unroll=True)

    column_products(0)
    pl.semaphore_wait(barrier, facets - 1 + strips - 1)

    def off_copy(d):
        return pltpu.make_async_remote_copy(
            src_ref=off_send,
            dst_ref=off_recv.at[f_me],
            send_sem=o_ssem.at[d - 1],
            recv_sem=o_rsem.at[d - 1],
            device_id=(facet_peers[d - 1], s_me),
            device_id_type=MESH,
        )

    def y_copy(c, d):
        return pltpu.make_async_remote_copy(
            src_ref=ysend.at[c, facet_peers[d - 1]],
            dst_ref=yrecv.at[c, f_me],
            send_sem=y_ssem.at[c, d - 1],
            recv_sem=y_rsem.at[c, d - 1],
            device_id=(facet_peers[d - 1], s_me),
            device_id_type=MESH,
        )

    def z_copy(c, d):
        return pltpu.make_async_remote_copy(
            src_ref=zsend.at[c, strip_peers[d - 1]],
            dst_ref=zrecv.at[c, d - 1],
            send_sem=z_ssem.at[c, d - 1],
            recv_sem=z_rsem.at[c, d - 1],
            device_id=(f_me, strip_peers[d - 1]),
            device_id_type=MESH,
        )

    off_copies = [off_copy(d) for d in range(1, facets)]
    for copy in off_copies:
        copy.start()

    y_copies = []
    for c in range(COLUMNS):
        if c > 0:
            column_products(c)

        def block(n, carry):
            re, im = row_block(n), im_block(n)
            pr, pi, qr, qi = pp[c, re], pp[c, im], qq[c, re], qq[c, im]
            gcr, gsr = gc_ref[re, c : c + 1], gs_ref[re, c : c + 1]
            halves = []
            for sign, yr, yi in ((0, pr + qi, pi - qr), (1, pr - qi, pi + qr)):
                at = 2 * c + sign
                hcr, hsr = hc[at : at + 1], hs[at : at + 1]
                a = gcr * hcr - gsr * hsr
                b = gcr * hsr + gsr * hcr
                halves.append(((yr * a + yi * b).astype(BF), (yi * a - yr * b).astype(BF)))
            for f in range(facets):
                if f >= facets // 2:
                    yr, yi = halves[0]
                    start = mb * f - half_m
                else:
                    yr, yi = halves[1]
                    start = half_m - mb * (f + 1)
                ysend[c, f, re] = jnp.concatenate(
                    [yr[:, start : start + mb], yi[:, start : start + mb]], axis=1
                )
            return carry

        lax.fori_loop(0, rows // BLOCK, block, 0, unroll=True)
        copies = [y_copy(c, d) for d in range(1, facets)]
        for d in spread_order(facets):
            copies[d - 1].start()
        y_copies.append(copies)
        yrecv[c, f_me] = ysend[c, f_me]

    for copy in off_copies:
        copy.wait_recv()
    rc_load.wait()
    rs_load.wait()
    offs = jnp.concatenate([off_recv[:, 0, :]] * (half_i // LANES), axis=1)
    phc, phs = cos_sin(
        (2 * iota((facets, half_i), 1) + 1) * (offs + s_me * rows), 2 * IMAGE_N
    )
    phc, phs = jnp.transpose(phc), jnp.transpose(phs)
    base_c, base_s = rc[...], rs[...]
    for f in range(facets):
        pc, ps = phc[:, f : f + 1], phs[:, f : f + 1]
        tc[:, f * rows : (f + 1) * rows] = (base_c * pc - base_s * ps).astype(BF)
        ts[:, f * rows : (f + 1) * rows] = (base_s * pc + base_c * ps).astype(BF)

    src, dst = iota((2 * mb, 2 * mb), 0), iota((2 * mb, 2 * mb), 1)
    same_part = (src >= mb) == (dst >= mb)
    mirrored = (src + dst - jnp.where(dst >= mb, 2 * mb, 0)) == mb - 1
    lower = jnp.where(f_me < facets // 2, 1, 0)
    picked = jnp.where(lower == 1, jnp.where(same_part & mirrored, 1, 0), jnp.where(src == dst, 1, 0))
    order = picked.astype(F32).astype(BF)

    z_copies = []
    for c in range(COLUMNS):
        for copy in y_copies[c]:
            copy.wait_recv()
        y = yrecv[c].reshape(facets * rows, 2 * mb)
        aa = dot(tc[...], y)
        bb = dot(ts[...], y)
        turned = jnp.concatenate([bb[:, mb:], -bb[:, :mb]], axis=1)
        upper_rows = dot((aa + turned).astype(BF), order).astype(BF)
        lower_rows = dot(flip, (aa - turned).astype(BF)).astype(BF)
        lower_rows = dot(lower_rows, order).astype(BF)
        z = jnp.concatenate([lower_rows, upper_rows], axis=0)
        zsend[c] = z.reshape(strips, ib, 2 * mb)
        copies = [z_copy(c, d) for d in range(1, strips)]
        for copy in reversed(copies):
            copy.start()
        z_copies.append(copies)

    totals = []
    for c in range(COLUMNS):
        total = zsend[c, s_me].astype(F32)
        for d in range(1, strips):
            z_copies[c][d - 1].wait_recv()
            total += zrecv[c, d - 1].astype(F32)
        totals.append(total)
    out_ref[...] = jnp.transpose(
        jnp.concatenate(
            [totals[0][:, :mb], totals[1][:, :mb], totals[0][:, mb:], totals[1][:, mb:]], axis=1
        )
    )
    for copy in off_copies + y_copies[0] + y_copies[1] + z_copies[0] + z_copies[1]:
        copy.wait_send()


def per_device(facet_pixels, facet_offsets, subgrid_offsets):
    rows, width = facet_pixels.shape[2], facet_pixels.shape[3]
    facets, strips = lax.axis_size("facet"), lax.axis_size("strip")
    mb, ib = FREQ // facets, ROW_FREQ // strips
    half_k, half_m, half_i = width // 2, FREQ // 2, ROW_FREQ // 2
    ct, st = (t.astype(ml_dtypes.bfloat16) for t in half_tables(half_k, half_m, 1))
    rc, rs = (
        np.ascontiguousarray(t.T.astype(np.float32)) for t in half_tables_rows(rows, half_i)
    )
    padded = -(-rows // LANES) * LANES
    loads = 2 * (half_k // CHUNK) + 2 * GROUPS + 4
    dma = pltpu.SemaphoreType.DMA
    flops = 2 * (4 * 2 * rows * half_k * half_m + 4 * half_i * facets * rows * 2 * mb)
    out = pl.pallas_call(
        functools.partial(kernel, facets, strips),
        out_shape=jax.ShapeDtypeStruct((4 * mb, ib), F32),
        in_specs=[pl.BlockSpec(memory_space=pltpu.HBM)] * 7,
        out_specs=pl.BlockSpec(memory_space=pltpu.VMEM),
        scratch_shapes=[
            pltpu.SMEM((1, 2), jnp.int32),
            pltpu.SMEM((COLUMNS, 2), jnp.int32),
            pltpu.VMEM((2, rows, width), BF),
            pltpu.VMEM((2 * rows, half_k), BF),
            pltpu.VMEM((half_k, half_m), BF),
            pltpu.VMEM((half_k, half_m), BF),
            pltpu.VMEM((half_i, rows), F32),
            pltpu.VMEM((half_i, rows), F32),
            pltpu.VMEM((COLUMNS, 2, 2 * rows, half_k), BF),
            pltpu.VMEM((padded, 8), F32),
            pltpu.VMEM((padded, 8), F32),
            pltpu.VMEM((COLUMNS, 2 * rows, half_m), F32),
            pltpu.VMEM((COLUMNS, 2 * rows, half_m), F32),
            pltpu.VMEM((COLUMNS, facets, rows, 2 * mb), BF),
            pltpu.VMEM((COLUMNS, facets, rows, 2 * mb), BF),
            pltpu.VMEM((half_i, facets * rows), BF),
            pltpu.VMEM((half_i, facets * rows), BF),
            pltpu.VMEM((8, LANES), jnp.int32),
            pltpu.VMEM((facets, 8, LANES), jnp.int32),
            pltpu.VMEM((COLUMNS, strips, ib, 2 * mb), BF),
            pltpu.VMEM((COLUMNS, strips - 1, ib, 2 * mb), BF),
            dma((loads,)),
            dma((COLUMNS, facets - 1)),
            dma((COLUMNS, facets - 1)),
            dma((facets - 1,)),
            dma((facets - 1,)),
            dma((COLUMNS, strips - 1)),
            dma((COLUMNS, strips - 1)),
        ],
        compiler_params=pltpu.CompilerParams(
            collective_id=0, has_side_effects=True, vmem_limit_bytes=63 * 1024 * 1024
        ),
        cost_estimate=pl.CostEstimate(
            flops=flops, bytes_accessed=4 * 1024 * 1024, transcendentals=0
        ),
    )(facet_offsets, subgrid_offsets, facet_pixels, ct, st, rc, rs)
    return jnp.transpose(out.reshape(2, COLUMNS, mb, ib), (3, 0, 1, 2))


def half_tables_rows(rows, half_i):
    r = np.arange(rows, dtype=np.int64)
    b = 2 * np.arange(half_i, dtype=np.int64) + 1
    t = (r[:, None] * b[None, :]) % (2 * IMAGE_N)
    angle = 2.0 * np.pi * t / (2 * IMAGE_N)
    return np.cos(angle), np.sin(angle)


def solution(mesh):
    in_specs = (P(None, "facet", "strip", None), P("facet", None), P())
    out_specs = P("strip", None, None, "facet")
    return jax.shard_map(
        per_device, mesh=mesh, in_specs=in_specs, out_specs=out_specs, check_vma=False
    )
```

```python
import functools
import math

import jax
import jax.numpy as jnp
import ml_dtypes
import numpy as np
from jax import lax
from jax.experimental import pallas as pl
from jax.experimental.pallas import tpu as pltpu
from jax.sharding import PartitionSpec as P

IMAGE_N = 65536
FREQ = 512
ROW_FREQ = 512
COLUMNS = 2
LANES = 128
CHUNK = 256
BLOCK = 16
GROUPS = 2
BF = jnp.bfloat16
F32 = jnp.float32
MESH = pl.DeviceIdType.MESH


def half_tables(count_a, count_b, step_a):
    a = 2 * np.arange(count_a, dtype=np.int64) + step_a
    b = 2 * np.arange(count_b, dtype=np.int64) + 1
    t = (a[:, None] * b[None, :]) % (4 * IMAGE_N)
    angle = 2.0 * np.pi * t / (4 * IMAGE_N)
    return np.cos(angle), np.sin(angle)


def cos_sin(product, modulus):
    t = (product + modulus // 2) & (modulus - 1)
    h = (t - modulus // 2).astype(F32) * (math.pi / modulus)
    h2 = h * h
    s = jnp.full_like(h, 1.0 / math.factorial(13))
    c = jnp.full_like(h, -1.0 / math.factorial(14))
    for n in range(11, 0, -2):
        s = s * h2 + (-1.0) ** ((n - 1) // 2) / math.factorial(n)
    for n in range(12, -1, -2):
        c = c * h2 + (-1.0) ** (n // 2) / math.factorial(n)
    s = s * h
    return 1.0 - 2.0 * s * s, 2.0 * s * c


def iota(shape, dim):
    return lax.broadcasted_iota(jnp.int32, shape, dim)


def dot(a, b):
    return jnp.dot(a, b, preferred_element_type=F32)


def kernel(
    facets, strips,
    fo_hbm, so_hbm, x_hbm, ct_hbm, st_hbm, rc_hbm, rs_hbm,
    out_ref,
    fo_ref, so_ref, x, xr, ct, st, rc, rs, evod, gc_ref, gs_ref, pp, qq, ysend, yrecv, tc, ts, off_send, off_recv, zsend, zrecv,
    load_sem, y_ssem, y_rsem, o_ssem, o_rsem, z_ssem, z_rsem,
):
    f_me = lax.axis_index("facet")
    s_me = lax.axis_index("strip")
    rows, width = x.shape[1], x.shape[2]
    half_k = width // 2
    half_m = FREQ // 2
    half_i = ROW_FREQ // 2
    mb = FREQ // facets
    ib = ROW_FREQ // strips
    chunks = half_k // CHUNK

    loads = []

    def load(src, dst):
        copy = pltpu.make_async_copy(src, dst, load_sem.at[len(loads)])
        copy.start()
        loads.append(copy)
        return copy

    fo_load = load(fo_hbm, fo_ref)
    so_load = load(so_hbm, so_ref)
    x_low, x_high, ct_load, st_load = [], [], [], []
    for g in range(GROUPS):
        for j in range(g * chunks // GROUPS, (g + 1) * chunks // GROUPS):
            low = pl.ds((chunks - 1 - j) * CHUNK, CHUNK)
            high = pl.ds(half_k + j * CHUNK, CHUNK)
            x_low.append(load(x_hbm.at[:, 0, :, low], x.at[:, :, low]))
            x_high.append(load(x_hbm.at[:, 0, :, high], x.at[:, :, high]))
        span = pl.ds(g * half_k // GROUPS, half_k // GROUPS)
        ct_load.append(load(ct_hbm.at[span], ct.at[span]))
        st_load.append(load(st_hbm.at[span], st.at[span]))
    rc_load = load(rc_hbm, rc)
    rs_load = load(rs_hbm, rs)

    facet_peers = [lax.rem(f_me + d, facets) for d in range(1, facets)]
    strip_peers = [lax.rem(s_me + d, strips) for d in range(1, strips)]
    barrier = pltpu.get_barrier_semaphore()
    for peer in facet_peers:
        pl.semaphore_signal(barrier, inc=1, device_id=(peer, s_me), device_id_type=MESH)
    for peer in strip_peers:
        pl.semaphore_signal(barrier, inc=1, device_id=(f_me, peer), device_id_type=MESH)

    fo_load.wait()
    so_load.wait()
    fx = fo_ref[0, 0]
    fy = fo_ref[0, 1]
    u0 = [so_ref[c, 0] for c in range(COLUMNS)]
    w0 = [so_ref[c, 1] for c in range(COLUMNS)]

    off_send[...] = jnp.full(off_send.shape, fy, jnp.int32)
    off_recv[f_me] = off_send[...]

    pieces = half_k // LANES
    a_index = iota((pieces, LANES), 0) * LANES + iota((pieces, LANES), 1)
    pq = [
        cos_sin((2 * a_index + 1) * (2 * u0[c] + (FREQ - 1)), 4 * IMAGE_N)
        for c in range(COLUMNS)
    ]

    row = iota((8, half_m), 0)
    lane = iota((8, half_m), 1)
    first = jnp.where(row < 2, u0[0], u0[1])
    freq = first + jnp.where((row & 1) == 0, half_m + lane, half_m - 1 - lane)
    hc, hs = cos_sin((2 * fx + (width - 1)) * freq, 2 * IMAGE_N)

    padded = -(-rows // LANES) * LANES
    row = iota((8, padded), 0)
    first = jnp.where(row == 0, w0[0], w0[1])
    pixel_row = s_me * rows + iota((8, padded), 1) + fy
    gc, gs = cos_sin((2 * first + (ROW_FREQ - 1)) * pixel_row, 2 * IMAGE_N)
    gc_ref[...] = jnp.transpose(gc)
    gs_ref[...] = jnp.transpose(gs)

    flip = (iota((CHUNK, CHUNK), 0) + iota((CHUNK, CHUNK), 1) == CHUNK - 1).astype(F32).astype(BF)

    def row_block(n):
        return pl.ds(pl.multiple_of(n * BLOCK, BLOCK), BLOCK)

    def im_block(n):
        return pl.ds(pl.multiple_of(rows + n * BLOCK, BLOCK), BLOCK)

    def column_products(c):
        per_group = chunks // GROUPS
        for g in range(GROUPS):
            group = range(g * per_group, (g + 1) * per_group)
            span = pl.ds(g * per_group * CHUNK, per_group * CHUNK)
            if c == 0:
                for j in group:
                    x_low[j].wait()
                    x_high[j].wait()
                for j in group:
                    low = x[:, :, pl.ds((chunks - 1 - j) * CHUNK, CHUNK)].reshape(2 * rows, CHUNK)
                    xr[:, pl.ds(j * CHUNK, CHUNK)] = dot(low, flip).astype(BF)
            for j in group:
                phase_chunk(c, j)
            if c == 0:
                ct_load[g].wait()
                st_load[g].wait()
            p_part = dot(evod[c, 0, :, span], ct[span])
            q_part = dot(evod[c, 1, :, span], st[span])
            pp[c] = p_part if g == 0 else pp[c] + p_part
            qq[c] = q_part if g == 0 else qq[c] + q_part

    def phase_chunk(c, j):
        cols = pl.ds(j * CHUNK, CHUNK)
        high_cols = pl.ds(half_k + j * CHUNK, CHUNK)
        first = j * (CHUNK // LANES)
        p, q = (
            jnp.concatenate(
                [part[first + n : first + n + 1] for n in range(CHUNK // LANES)], axis=1
            )
            for part in pq[c]
        )

        def block(n, carry):
            re, im = row_block(n), im_block(n)
            hr, hi = x[0, re, high_cols].astype(F32), x[1, re, high_cols].astype(F32)
            lr, li = xr[re, cols].astype(F32), xr[im, cols].astype(F32)
            er, odr, ei, odi = hr + lr, hr - lr, hi + li, hi - li
            evod[c, 0, re, cols] = (er * p + odi * q).astype(BF)
            evod[c, 0, im, cols] = (ei * p - odr * q).astype(BF)
            evod[c, 1, re, cols] = (odr * p + ei * q).astype(BF)
            evod[c, 1, im, cols] = (odi * p - er * q).astype(BF)
            return carry

        lax.fori_loop(0, rows // BLOCK, block, 0, unroll=True)

    column_products(0)
    pl.semaphore_wait(barrier, facets - 1 + strips - 1)

    def off_copy(d):
        return pltpu.make_async_remote_copy(
            src_ref=off_send,
            dst_ref=off_recv.at[f_me],
            send_sem=o_ssem.at[d - 1],
            recv_sem=o_rsem.at[d - 1],
            device_id=(facet_peers[d - 1], s_me),
            device_id_type=MESH,
        )

    def y_copy(c, d):
        return pltpu.make_async_remote_copy(
            src_ref=ysend.at[c, facet_peers[d - 1]],
            dst_ref=yrecv.at[c, f_me],
            send_sem=y_ssem.at[c, d - 1],
            recv_sem=y_rsem.at[c, d - 1],
            device_id=(facet_peers[d - 1], s_me),
            device_id_type=MESH,
        )

    def z_copy(c, d):
        return pltpu.make_async_remote_copy(
            src_ref=zsend.at[c, strip_peers[d - 1]],
            dst_ref=zrecv.at[c, d - 1],
            send_sem=z_ssem.at[c, d - 1],
            recv_sem=z_rsem.at[c, d - 1],
            device_id=(f_me, strip_peers[d - 1]),
            device_id_type=MESH,
        )

    off_copies = [off_copy(d) for d in range(1, facets)]
    for copy in off_copies:
        copy.start()

    y_copies = []
    for c in range(COLUMNS):
        if c > 0:
            column_products(c)

        def block(n, carry):
            re, im = row_block(n), im_block(n)
            pr, pi, qr, qi = pp[c, re], pp[c, im], qq[c, re], qq[c, im]
            gcr, gsr = gc_ref[re, c : c + 1], gs_ref[re, c : c + 1]
            halves = []
            for sign, yr, yi in ((0, pr + qi, pi - qr), (1, pr - qi, pi + qr)):
                at = 2 * c + sign
                hcr, hsr = hc[at : at + 1], hs[at : at + 1]
                a = gcr * hcr - gsr * hsr
                b = gcr * hsr + gsr * hcr
                halves.append(((yr * a + yi * b).astype(BF), (yi * a - yr * b).astype(BF)))
            for f in range(facets):
                if f >= facets // 2:
                    yr, yi = halves[0]
                    start = mb * f - half_m
                else:
                    yr, yi = halves[1]
                    start = half_m - mb * (f + 1)
                ysend[c, f, re] = jnp.concatenate(
                    [yr[:, start : start + mb], yi[:, start : start + mb]], axis=1
                )
            return carry

        lax.fori_loop(0, rows // BLOCK, block, 0, unroll=True)
        copies = [y_copy(c, d) for d in range(1, facets)]
        for copy in copies:
            copy.start()
        y_copies.append(copies)
        yrecv[c, f_me] = ysend[c, f_me]

    for copy in off_copies:
        copy.wait_recv()
    rc_load.wait()
    rs_load.wait()
    offs = jnp.concatenate([off_recv[:, 0, :]] * (half_i // LANES), axis=1)
    phc, phs = cos_sin(
        (2 * iota((facets, half_i), 1) + 1) * (offs + s_me * rows), 2 * IMAGE_N
    )
    phc, phs = jnp.transpose(phc), jnp.transpose(phs)
    base_c, base_s = rc[...], rs[...]
    for f in range(facets):
        pc, ps = phc[:, f : f + 1], phs[:, f : f + 1]
        tc[:, f * rows : (f + 1) * rows] = (base_c * pc - base_s * ps).astype(BF)
        ts[:, f * rows : (f + 1) * rows] = (base_s * pc + base_c * ps).astype(BF)

    src, dst = iota((2 * mb, 2 * mb), 0), iota((2 * mb, 2 * mb), 1)
    same_part = (src >= mb) == (dst >= mb)
    mirrored = (src + dst - jnp.where(dst >= mb, 2 * mb, 0)) == mb - 1
    lower = jnp.where(f_me < facets // 2, 1, 0)
    picked = jnp.where(lower == 1, jnp.where(same_part & mirrored, 1, 0), jnp.where(src == dst, 1, 0))
    order = picked.astype(F32).astype(BF)

    z_copies = []
    for c in range(COLUMNS):
        for copy in y_copies[c]:
            copy.wait_recv()
        y = yrecv[c].reshape(facets * rows, 2 * mb)
        aa = dot(tc[...], y)
        bb = dot(ts[...], y)
        turned = jnp.concatenate([bb[:, mb:], -bb[:, :mb]], axis=1)
        half_s = strips // 2
        upper_rows = dot((aa + turned).astype(BF), order).astype(BF)
        lower_rows = dot(flip, (aa - turned).astype(BF)).astype(BF)
        lower_rows = dot(lower_rows, order).astype(BF)
        zsend[c, half_s:] = upper_rows.reshape(half_s, ib, 2 * mb)
        zsend[c, :half_s] = lower_rows.reshape(half_s, ib, 2 * mb)
        copies = [z_copy(c, d) for d in range(1, strips)]
        for copy in copies:
            copy.start()
        z_copies.append(copies)

    totals = []
    for c in range(COLUMNS):
        total = zsend[c, s_me].astype(F32)
        for d in range(1, strips):
            z_copies[c][d - 1].wait_recv()
            total += zrecv[c, d - 1].astype(F32)
        totals.append(total)
    out_ref[...] = jnp.transpose(
        jnp.concatenate(
            [totals[0][:, :mb], totals[1][:, :mb], totals[0][:, mb:], totals[1][:, mb:]], axis=1
        )
    )
    for copy in off_copies + y_copies[0] + y_copies[1] + z_copies[0] + z_copies[1]:
        copy.wait_send()


def per_device(facet_pixels, facet_offsets, subgrid_offsets):
    rows, width = facet_pixels.shape[2], facet_pixels.shape[3]
    facets, strips = lax.axis_size("facet"), lax.axis_size("strip")
    mb, ib = FREQ // facets, ROW_FREQ // strips
    half_k, half_m, half_i = width // 2, FREQ // 2, ROW_FREQ // 2
    ct, st = (t.astype(ml_dtypes.bfloat16) for t in half_tables(half_k, half_m, 1))
    rc, rs = (
        np.ascontiguousarray(t.T.astype(np.float32)) for t in half_tables_rows(rows, half_i)
    )
    padded = -(-rows // LANES) * LANES
    loads = 2 * (half_k // CHUNK) + 2 * GROUPS + 4
    dma = pltpu.SemaphoreType.DMA
    flops = 2 * (4 * 2 * rows * half_k * half_m + 4 * half_i * facets * rows * 2 * mb)
    out = pl.pallas_call(
        functools.partial(kernel, facets, strips),
        out_shape=jax.ShapeDtypeStruct((4 * mb, ib), F32),
        in_specs=[pl.BlockSpec(memory_space=pltpu.HBM)] * 7,
        out_specs=pl.BlockSpec(memory_space=pltpu.VMEM),
        scratch_shapes=[
            pltpu.SMEM((1, 2), jnp.int32),
            pltpu.SMEM((COLUMNS, 2), jnp.int32),
            pltpu.VMEM((2, rows, width), BF),
            pltpu.VMEM((2 * rows, half_k), BF),
            pltpu.VMEM((half_k, half_m), BF),
            pltpu.VMEM((half_k, half_m), BF),
            pltpu.VMEM((half_i, rows), F32),
            pltpu.VMEM((half_i, rows), F32),
            pltpu.VMEM((COLUMNS, 2, 2 * rows, half_k), BF),
            pltpu.VMEM((padded, 8), F32),
            pltpu.VMEM((padded, 8), F32),
            pltpu.VMEM((COLUMNS, 2 * rows, half_m), F32),
            pltpu.VMEM((COLUMNS, 2 * rows, half_m), F32),
            pltpu.VMEM((COLUMNS, facets, rows, 2 * mb), BF),
            pltpu.VMEM((COLUMNS, facets, rows, 2 * mb), BF),
            pltpu.VMEM((half_i, facets * rows), BF),
            pltpu.VMEM((half_i, facets * rows), BF),
            pltpu.VMEM((8, LANES), jnp.int32),
            pltpu.VMEM((facets, 8, LANES), jnp.int32),
            pltpu.VMEM((COLUMNS, strips, ib, 2 * mb), BF),
            pltpu.VMEM((COLUMNS, strips - 1, ib, 2 * mb), BF),
            dma((loads,)),
            dma((COLUMNS, facets - 1)),
            dma((COLUMNS, facets - 1)),
            dma((facets - 1,)),
            dma((facets - 1,)),
            dma((COLUMNS, strips - 1)),
            dma((COLUMNS, strips - 1)),
        ],
        compiler_params=pltpu.CompilerParams(
            collective_id=0, has_side_effects=True, vmem_limit_bytes=63 * 1024 * 1024
        ),
        cost_estimate=pl.CostEstimate(
            flops=flops, bytes_accessed=4 * 1024 * 1024, transcendentals=0
        ),
    )(facet_offsets, subgrid_offsets, facet_pixels, ct, st, rc, rs)
    scale = 1.0 / math.sqrt(width * rows * strips * facets)
    return jnp.transpose(scale * out.reshape(2, COLUMNS, mb, ib), (3, 0, 1, 2))


def half_tables_rows(rows, half_i):
    r = np.arange(rows, dtype=np.int64)
    b = 2 * np.arange(half_i, dtype=np.int64) + 1
    t = (r[:, None] * b[None, :]) % (2 * IMAGE_N)
    angle = 2.0 * np.pi * t / (2 * IMAGE_N)
    return np.cos(angle), np.sin(angle)


def solution(mesh):
    in_specs = (P(None, "facet", "strip", None), P("facet", None), P())
    out_specs = P("strip", None, None, "facet")
    return jax.shard_map(
        per_device, mesh=mesh, in_specs=in_specs, out_specs=out_specs, check_vma=False
    )
```
